512 devices in a mesh: dp: 64 (over x, z, y_lo), tensor: 8 (over y_hi, core).
Axes of the slice: x: 4, y: 8 (y_hi: 4, y_lo: 2; y = y_hi * 2 + y_lo), z: 8, core: 2. Of those that a mesh axis runs over, the one named last changes fastest.
Arguments:
- pooled: bfloat16 [8192, 1536], P('dp', 'tensor'), may hold values from -16 to 16
- ln_gain: float32 [1536], replicated, may hold values from 0.5 to 1.5
- ln_bias: float32 [1536], replicated, may hold values from -4 to 4
- w_up: bfloat16 [1536, 3072], P(None, 'tensor'), may hold values from -0.15625 to 0.15625
- b_up: float32 [3072], P('tensor'), may hold values from -4 to 4
- w_down: bfloat16 [3072, 1536], P('tensor'), may hold values from -0.21875 to 0.21875
- b_down: float32 [1536], P('tensor'), may hold values from -4 to 4
- text_embed: bfloat16 [8192, 1536], P('dp', 'tensor'), may hold values from -16 to 16
- image_ids: int32 [8192], P('dp'), may hold values from 0 to 8191, as said below
- text_ids: int32 [8192], P('dp'), may hold values from 0 to 8191, as said below
- logit_scale: float32 [1], replicated, may hold values from 9 to 11
- logit_bias: float32 [1], replicated, may hold values from -10.5 to -9.5
- loss_scale: float32 [1], replicated, may hold values from 524288 to 2097152
Outputs:
- loss: float32 [1], replicated
- grad_pooled: bfloat16 [8192, 1536], P('dp', 'tensor')
- grad_down: float32 [3072, 1536], P('tensor', 'dp')
The draws below stay inside these ranges and needn't reach their ends.
Inputs may be any that keep to these rules, and one draw needn't show every extreme that they name: `image_ids`: each holds every pair id of the batch exactly once, so each image has exactly one positive text. `text_ids`: each holds every pair id of the batch exactly once.
All inputs are finite; a program needn't handle non-finite values.
Results may differ from the reference program's by a relative error of at most 0.0074.
The reference program's roundings to bfloat16 on the way (of `normed`, `hidden`, `weights`, `grad_low` and `grad_pre`) count: a program that leaves them out, or rounds other values in their place, can miss the bound.
Values may be sent and summed in bfloat16 or wider, within the bound.
No kernel may reach another device: no remote copies, remote signals or barrier semaphores. Data moves between devices by JAX's collectives and lax.ppermute only.
A program may use at most 128 MiB of HBM per device.

```python
import math
import jax
import jax.numpy as jnp
from jax import lax

D = 1536
FF = 3072
IMG_DEV = 128
BATCH = 8192
N_DP = 64


def pair_orders(key):
    first = jax.random.permutation(jax.random.fold_in(key, 101), BATCH).astype(jnp.int32)
    second = jax.random.permutation(jax.random.fold_in(key, 102), BATCH).astype(jnp.int32)
    return (first, second)


def shared_basis(key):
    basis = jax.random.normal(jax.random.fold_in(key, 103), (5, D), jnp.float32)
    latent = jax.random.normal(jax.random.fold_in(key, 104), (BATCH, 4), jnp.float32)
    return (basis, latent)


def mix_rows(basis, mixing):
    total = mixing[:, 0:1] * basis[0][None, :]
    for column in range(1, 4):
        total = total + mixing[:, column:column + 1] * basis[column][None, :]
    return 0.5 * total


def draw_image_ids(key, part):
    first, second = pair_orders(key)
    return first


def draw_text_ids(key, part):
    first, second = pair_orders(key)
    return second


def draw_pooled(key, part):
    first, second = pair_orders(key)
    basis, latent = shared_basis(key)
    key = jax.random.fold_in(key, 3)
    keys = jax.random.split(key, 2)
    mixing = latent[first] + 0.5 * jax.random.normal(keys[0], (BATCH, 4), jnp.float32)
    signal = mix_rows(basis, mixing)
    rows = signal + 0.7 * jax.random.normal(keys[1], (BATCH, D), jnp.float32)
    return jnp.clip(rows, -16.0, 16.0).astype(jnp.bfloat16)


def draw_text_embed(key, part):
    first, second = pair_orders(key)
    basis, latent = shared_basis(key)
    key = jax.random.fold_in(key, 4)
    keys = jax.random.split(key, 2)
    mixing = latent[second] + 0.5 * jax.random.normal(keys[0], (BATCH, 4), jnp.float32)
    signal = mix_rows(basis, mixing)
    rows = signal + 0.7 * jax.random.normal(keys[1], (BATCH, D), jnp.float32)
    return jnp.clip(rows, -16.0, 16.0).astype(jnp.bfloat16)


def level_of(key, extent, cuts, least, largest):
    loudness = 1.0
    for dim, shards_of in cuts:
        steps = jax.random.uniform(jax.random.fold_in(jax.random.fold_in(key, 6), dim), (shards_of,), jnp.float32, least / len(cuts), largest / len(cuts))
        loudness = loudness * jnp.repeat(jnp.exp(steps), extent[dim] // shards_of).reshape((-1,) + (1,) * (len(extent) - 1 - dim))
    return loudness


def normal_values(key, dims, scale, most, pieces=(), kind=jnp.bfloat16):
    drawn = jax.random.normal(key, dims, jnp.float32) * scale
    if len(pieces) > 0:
        drawn = level_of(key, dims, pieces, -0.22, 0.18) * drawn
    return jnp.clip(drawn, min=-most, max=most).astype(kind)


def setup_inputs(seed: int = 0) -> dict:
    key_list = jax.random.split(jax.random.key(seed), 14)
    pooled = draw_pooled(jax.random.fold_in(key_list[13], 71), 0)
    ln_gain = jnp.clip(1.0 + 0.1 * jax.random.normal(key_list[1], (D,), jnp.float32), 0.5, 1.5)
    ln_bias = normal_values(key_list[2], (D,), 1.0, 4.0, (), jnp.float32)
    w_up = normal_values(key_list[3], (D, FF), D ** -0.5, 0.15625, ((1, 8),))
    b_up = normal_values(key_list[4], (FF,), 1.0, 4.0, ((0, 8),), jnp.float32)
    w_down = normal_values(key_list[5], (FF, D), (FF // 4) ** -0.5, 0.21875, ((0, 8),))
    b_down = normal_values(key_list[6], (D,), 1.0, 4.0, ((0, 8),), jnp.float32)
    text_embed = draw_text_embed(jax.random.fold_in(key_list[13], 71), 0)
    image_ids = draw_image_ids(jax.random.fold_in(key_list[13], 71), 0)
    text_ids = draw_text_ids(jax.random.fold_in(key_list[13], 71), 0)
    logit_scale = jnp.clip(jax.random.uniform(key_list[10], (1,), jnp.float32, 9.0, 11.0), 9.0, 11.0)
    logit_bias = jnp.clip(jax.random.uniform(key_list[11], (1,), jnp.float32, -10.5, -9.5), -10.5, -9.5)
    loss_scale = jnp.clip(jnp.exp(jax.random.uniform(key_list[12], (1,), jnp.float32, math.log(524288.0), math.log(2097152))), 524288.0, 2097152)
    return {"pooled": pooled, "ln_gain": ln_gain, "ln_bias": ln_bias, "w_up": w_up, "b_up": b_up, "w_down": w_down, "b_down": b_down, "text_embed": text_embed, "image_ids": image_ids, "text_ids": text_ids, "logit_scale": logit_scale, "logit_bias": logit_bias, "loss_scale": loss_scale}


def gelu_fn(values):
    return jax.nn.gelu(values, approximate=True)

def normalize_rows(rows):
    wide = rows.astype(jnp.float32)
    average = lax.optimization_barrier(jnp.mean(wide, axis=1, keepdims=True))
    centered = wide - average
    inverse = lax.rsqrt(lax.optimization_barrier(jnp.mean(centered * centered, axis=1, keepdims=True)) + 1e-06)
    return (centered * inverse, inverse)

def reference(pooled, ln_gain, ln_bias, w_up, b_up, w_down, b_down, text_embed, image_ids, text_ids, logit_scale, logit_bias, loss_scale):
    scaled, inverse = normalize_rows(pooled)
    normed = (scaled * ln_gain + ln_bias).astype(jnp.bfloat16)
    preact = jnp.dot(normed, w_up, preferred_element_type=jnp.float32) + b_up
    hidden = gelu_fn(preact).astype(jnp.bfloat16)
    summed = pooled.astype(jnp.float32) + jnp.dot(hidden, w_down, preferred_element_type=jnp.float32) + b_down
    img_norm = jnp.sqrt(lax.optimization_barrier(jnp.sum(summed * summed, axis=1, keepdims=True)) + 1e-06)
    img_unit = summed / img_norm
    img_low = img_unit.astype(jnp.bfloat16)
    txt_wide = text_embed.astype(jnp.float32)
    txt_low = (txt_wide / jnp.sqrt(lax.optimization_barrier(jnp.sum(txt_wide * txt_wide, axis=1, keepdims=True)) + 1e-06)).astype(jnp.bfloat16)
    temper = logit_scale[0]
    offset = logit_bias[0]
    factor = loss_scale[0] / BATCH

    def one_block(index):
        start = index * IMG_DEV
        img_rows = lax.dynamic_slice_in_dim(img_low, start, IMG_DEV, 0)
        row_ids = lax.dynamic_slice_in_dim(image_ids, start, IMG_DEV, 0)
        scores = jnp.dot(img_rows, txt_low.T, preferred_element_type=jnp.float32)
        positive = row_ids[:, None] == text_ids[None, :]
        signs = jnp.where(positive, 1.0, -1.0).astype(jnp.float32)
        logits = temper * scores + offset
        margin = -signs * logits
        row_loss = lax.optimization_barrier(jnp.sum(jax.nn.softplus(margin), axis=1))
        weights = (-signs * temper * factor * jax.nn.sigmoid(margin)).astype(jnp.bfloat16)
        grad_block = jnp.dot(weights, txt_low, preferred_element_type=jnp.float32)
        return (row_loss, grad_block)
    row_loss, grad_unit = lax.map(one_block, jnp.arange(N_DP, dtype=jnp.int32))
    loss = (jnp.sum(row_loss) / BATCH).reshape(1)
    grad_unit = grad_unit.reshape(BATCH, D)
    tangent = lax.optimization_barrier(jnp.sum(img_unit * grad_unit, axis=1, keepdims=True))
    grad_sum = (grad_unit - img_unit * tangent) / img_norm
    grad_low = grad_sum.astype(jnp.bfloat16)
    grad_down = jnp.dot(hidden.T, grad_low, preferred_element_type=jnp.float32)
    grad_hidden = jnp.dot(grad_low, w_down.T, preferred_element_type=jnp.float32)
    grad_pre = jax.vjp(gelu_fn, preact)[1](grad_hidden)[0].astype(jnp.bfloat16)
    grad_normed = jnp.dot(grad_pre, w_up.T, preferred_element_type=jnp.float32)
    scaled_grad = grad_normed * ln_gain
    centre = lax.optimization_barrier(jnp.mean(scaled_grad, axis=1, keepdims=True))
    along = lax.optimization_barrier(jnp.mean(scaled_grad * scaled, axis=1, keepdims=True))
    grad_input = inverse * (scaled_grad - centre - scaled * along)
    grad_pooled = (grad_sum + grad_input).astype(jnp.bfloat16)
    return (loss, grad_pooled, grad_down)
```

```python
import jax
import jax.numpy as jnp
from jax import lax
from jax.sharding import Mesh, PartitionSpec as P

ROWS = 128
WIDE = 1536
SLICE = 192
EXTRA = 128
IMG = 16
DATA = ("x", "z", "ylo")
TENS = ("yhi", "core")
RING = ("ylo", "yhi", "core")
DIGITS = 8
SPAN = 2.0**26


def gelu_fn(values):
    return jax.nn.gelu(values, approximate=True)


def id_columns(ids):
    high = (ids // 128).astype(jnp.bfloat16)
    low = (ids % 128).astype(jnp.bfloat16)
    pair = jnp.stack([high, low], axis=1)
    return jnp.pad(pair, ((0, 0), (0, EXTRA - 2)))


def read_ids(block):
    wide = block[:, WIDE : WIDE + 2].astype(jnp.float32)
    return wide[:, 0] * 128.0 + wide[:, 1]


def to_digits(value):
    rest = value / SPAN
    digits = []
    for _ in range(DIGITS):
        rest = rest * 64.0
        digit = jnp.floor(rest)
        rest = rest - digit
        digits.append(digit)
    return jnp.stack(digits)


def from_digits(digits):
    total = jnp.float32(0.0)
    for place in range(DIGITS):
        total = total + digits[place] * (SPAN / 64.0 ** (place + 1))
    return total


def halves(values):
    high = values.astype(jnp.bfloat16)
    low = (values - high.astype(jnp.float32)).astype(jnp.bfloat16)
    return high, low


def shards(
    pooled,
    ln_gain,
    ln_bias,
    w_up,
    b_up,
    w_down,
    b_down,
    text_embed,
    image_ids,
    text_ids,
    logit_scale,
    logit_bias,
    loss_scale,
):
    tens = lax.axis_index(TENS)
    row0 = tens * IMG
    col0 = tens * SLICE
    batch = ROWS * 64

    both = lax.all_gather(
        jnp.concatenate([pooled, text_embed], axis=0), TENS, axis=1, tiled=True
    )
    txt_rows = lax.dynamic_slice_in_dim(both, ROWS + row0, IMG, 0).astype(jnp.float32)
    txt_norm = jnp.sqrt(jnp.sum(txt_rows * txt_rows, axis=1, keepdims=True) + 1e-06)
    txt_low = (txt_rows / txt_norm).astype(jnp.bfloat16)
    txt_ids = lax.dynamic_slice_in_dim(text_ids, row0, IMG, 0)
    txt_send = jnp.concatenate([txt_low, id_columns(txt_ids)], axis=1)
    txt_x = lax.all_gather(txt_send, "x", axis=0, tiled=True)
    txt_x, both = lax.optimization_barrier((txt_x, both))
    txt_all = lax.all_gather(txt_x, "z", axis=0, tiled=True)

    wide = both[:ROWS].astype(jnp.float32)
    average = jnp.mean(wide, axis=1, keepdims=True)
    centered = wide - average
    inverse = lax.rsqrt(jnp.mean(centered * centered, axis=1, keepdims=True) + 1e-06)
    scaled = centered * inverse
    normed = (scaled * ln_gain + ln_bias).astype(jnp.bfloat16)
    preact = jnp.dot(normed, w_up, preferred_element_type=jnp.float32) + b_up
    hidden = gelu_fn(preact).astype(jnp.bfloat16)
    bias_row = lax.dynamic_update_slice_in_dim(
        jnp.zeros((WIDE,), jnp.float32), b_down, col0, 0
    )
    part = jnp.dot(hidden, w_down, preferred_element_type=jnp.float32) + bias_row
    parts = lax.all_to_all(
        part.astype(jnp.bfloat16), TENS, split_axis=0, concat_axis=0, tiled=True
    )
    mixed = jnp.sum(parts.reshape(8, IMG, WIDE).astype(jnp.float32), axis=0)
    own = lax.dynamic_slice_in_dim(both, row0, IMG, 0).astype(jnp.float32)
    summed = own + mixed
    img_norm = jnp.sqrt(jnp.sum(summed * summed, axis=1, keepdims=True) + 1e-06)
    img_unit = summed / img_norm
    img_ids = lax.dynamic_slice_in_dim(image_ids, row0, IMG, 0)
    img_send = jnp.concatenate([img_unit.astype(jnp.bfloat16), id_columns(img_ids)], axis=1)
    img_all = lax.all_gather(img_send, RING, axis=0, tiled=True)

    temper = logit_scale[0]
    offset = logit_bias[0]
    factor = loss_scale[0] / batch
    txt_full = txt_all[:, :WIDE]
    scores = lax.dot_general(
        img_all[:, :WIDE], txt_full, (((1,), (1,)), ((), ())), preferred_element_type=jnp.float32
    )
    positive = read_ids(img_all)[:, None] == read_ids(txt_all)[None, :]
    signs = jnp.where(positive, 1.0, -1.0).astype(jnp.float32)
    margin = -signs * (temper * scores + offset)
    loss_part = jnp.sum(jax.nn.softplus(margin))
    weights = (-signs * temper * factor * jax.nn.sigmoid(margin)).astype(jnp.bfloat16)
    unit_part = jnp.dot(weights, txt_full, preferred_element_type=jnp.float32)
    unit_parts = lax.all_to_all(
        unit_part.astype(jnp.bfloat16), RING, split_axis=0, concat_axis=0, tiled=True
    )
    grad_unit = jnp.sum(unit_parts.reshape(16, IMG, WIDE).astype(jnp.float32), axis=0)
    tangent = jnp.sum(img_unit * grad_unit, axis=1, keepdims=True)
    grad_low = ((grad_unit - img_unit * tangent) / img_norm).astype(jnp.bfloat16)
    loss_row = jnp.pad(to_digits(loss_part).astype(jnp.bfloat16), (0, EXTRA - DIGITS))
    grad_send = jnp.concatenate([grad_low, jnp.broadcast_to(loss_row, (IMG, EXTRA))], axis=1)
    grad_all = lax.all_gather(grad_send, TENS, axis=0, tiled=True)
    grad_full = grad_all[:, :WIDE]

    group_digits = jnp.sum(
        grad_all.reshape(8, IMG, WIDE + EXTRA)[:, 0, WIDE : WIDE + DIGITS].astype(jnp.float32), axis=0
    )
    group_loss = from_digits(group_digits)
    down_part = lax.dot_general(
        grad_full, hidden, (((0,), (0,)), ((), ())), preferred_element_type=jnp.float32
    ).astype(jnp.bfloat16)
    loss_block = jnp.zeros((16, 384), jnp.bfloat16) + jnp.pad(
        to_digits(group_loss).astype(jnp.bfloat16), (0, 384 - DIGITS)
    )
    down_send = jnp.concatenate(
        [down_part.reshape(4, 384, 384), jnp.broadcast_to(loss_block, (4, 16, 384))], axis=1
    ).reshape(1600, 384)
    down_x = lax.psum_scatter(down_send, "x", scatter_dimension=0, tiled=True)

    grad_hidden = lax.dot_general(
        grad_full, w_down, (((1,), (1,)), ((), ())), preferred_element_type=jnp.float32
    )
    grad_pre = jax.vjp(gelu_fn, preact)[1](grad_hidden)[0].astype(jnp.bfloat16)
    normed_part = lax.dot_general(
        w_up, grad_pre, (((1,), (1,)), ((), ())), preferred_element_type=jnp.float32
    )
    gained = normed_part * ln_gain[:, None]
    sum_h = jnp.sum(gained, axis=0)
    sum_hs = jnp.sum(gained * scaled.T, axis=0)
    h_hi, h_lo = halves(sum_h)
    s_hi, s_lo = halves(sum_hs)
    stats = jnp.pad(jnp.stack([h_hi, h_lo, s_hi, s_lo]), ((0, 12), (0, 0)))
    norm_send = jnp.concatenate(
        [
            normed_part.astype(jnp.bfloat16).reshape(8, SLICE, ROWS),
            jnp.broadcast_to(stats, (8, 16, ROWS)),
        ],
        axis=1,
    )
    norm_parts = lax.all_to_all(norm_send, TENS, split_axis=0, concat_axis=0, tiled=True)
    norm_sum = jnp.sum(norm_parts.astype(jnp.float32), axis=0)
    centre = (norm_sum[SLICE] + norm_sum[SLICE + 1]) / WIDE
    along = (norm_sum[SLICE + 2] + norm_sum[SLICE + 3]) / WIDE
    gain_own = lax.dynamic_slice_in_dim(ln_gain, col0, SLICE, 0)
    scaled_own = (pooled.astype(jnp.float32) - average) * inverse
    h_own = norm_sum[:SLICE].T * gain_own[None, :]
    grad_own = lax.dynamic_slice_in_dim(grad_full, col0, SLICE, 1).astype(jnp.float32)
    grad_input = inverse * (h_own - centre[:, None] - scaled_own * along[:, None])
    grad_pooled = (grad_own + grad_input).astype(jnp.bfloat16)

    digits_x = down_x[384, :DIGITS].astype(jnp.float32)
    loss_x = from_digits(digits_x)
    loss_tail = jnp.pad(
        jnp.stack([*three(loss_x)]), (0, 384 - 3)
    )
    last_send = jnp.concatenate(
        [
            down_x[:384].reshape(16, 24, 384),
            jnp.broadcast_to(loss_tail, (16, 8, 384)),
        ],
        axis=1,
    )
    last = lax.all_to_all(last_send, ("z", "ylo"), split_axis=0, concat_axis=0, tiled=True)
    last_sum = jnp.sum(last.astype(jnp.float32), axis=0)
    grad_down = last_sum[:24].T
    loss = (jnp.sum(last_sum[24, :3]) / batch).reshape(1)
    return (loss, grad_pooled, grad_down)


def three(value):
    first = value.astype(jnp.bfloat16)
    rest = value - first.astype(jnp.float32)
    second = rest.astype(jnp.bfloat16)
    third = (rest - second.astype(jnp.float32)).astype(jnp.bfloat16)
    return first, second, third


def solution(mesh):
    inner = Mesh(mesh.devices.reshape(4, 8, 2, 4, 2), ("x", "z", "ylo", "yhi", "core"))
    placed = (
        P(DATA, TENS),
        P(),
        P(),
        P(None, TENS),
        P(TENS),
        P(TENS, None),
        P(TENS),
        P(DATA, TENS),
        P(DATA),
        P(DATA),
        P(),
        P(),
        P(),
    )
    return jax.shard_map(
        shards,
        mesh=inner,
        in_specs=placed,
        out_specs=(P(), P(DATA, TENS), P(TENS, DATA)),
        check_vma=False,
    )
```

```python
import jax
import jax.numpy as jnp
from jax import lax
from jax.sharding import Mesh, PartitionSpec as P

ROWS = 128
WIDE = 1536
SLICE = 192
EXTRA = 128
IMG = 16
DATA = ("x", "z", "ylo")
TENS = ("yhi", "core")
RING = ("ylo", "yhi", "core")
LANES = 64
DIGITS = 16
SPAN = 2.0**16


def gelu_fn(values):
    return jax.nn.gelu(values, approximate=True)


def id_columns(ids):
    high = (ids // 128).astype(jnp.bfloat16)
    low = (ids % 128).astype(jnp.bfloat16)
    pair = jnp.stack([high, low], axis=1)
    return jnp.pad(pair, ((0, 0), (0, EXTRA - 2)))


def read_ids(block):
    wide = block[:, WIDE : WIDE + 2].astype(jnp.float32)
    return wide[:, 0] * 128.0 + wide[:, 1]


def to_digits(values):
    places = 4.0 ** jnp.arange(1, DIGITS + 1, dtype=jnp.float32)[:, None]
    upper = jnp.floor(values[None, :] * (places / SPAN))
    lower = jnp.floor(values[None, :] * (places / (4.0 * SPAN)))
    return (upper - 4.0 * lower).astype(jnp.bfloat16)


def from_digits(digits):
    places = SPAN / 4.0 ** jnp.arange(1, DIGITS + 1, dtype=jnp.float32)[:, None]
    return jnp.sum(digits.astype(jnp.float32) * places, axis=0)


def pieces(values, count):
    parts = []
    for _ in range(count):
        part = lax.reduce_precision(values, 8, 7)
        parts.append(part.astype(jnp.bfloat16))
        values = values - part
    return jnp.stack(parts)


def spread(block, axis, count):
    send = jnp.broadcast_to(block[None], (count,) + block.shape)
    return lax.all_to_all(send, axis, split_axis=0, concat_axis=0, tiled=True).reshape(
        count * block.shape[0], block.shape[1]
    )


def shards(
    pooled,
    ln_gain,
    ln_bias,
    w_up,
    b_up,
    w_down,
    b_down,
    text_embed,
    image_ids,
    text_ids,
    logit_scale,
    logit_bias,
    loss_scale,
):
    tens = lax.axis_index(TENS)
    row0 = tens * IMG
    col0 = tens * SLICE
    batch = ROWS * 64

    both = lax.all_gather(
        jnp.concatenate([pooled, text_embed], axis=0), TENS, axis=1, tiled=True
    )
    txt_rows = lax.dynamic_slice_in_dim(both, ROWS + row0, IMG, 0).astype(jnp.float32)
    txt_norm = jnp.sqrt(jnp.sum(txt_rows * txt_rows, axis=1, keepdims=True) + 1e-06)
    txt_low = (txt_rows / txt_norm).astype(jnp.bfloat16)
    txt_ids = lax.dynamic_slice_in_dim(text_ids, row0, IMG, 0)
    txt_x = spread(jnp.concatenate([txt_low, id_columns(txt_ids)], axis=1), "x", 4)
    txt_all = lax.all_gather(txt_x, "z", axis=0, tiled=True)

    wide = both[:ROWS].astype(jnp.float32)
    average = jnp.mean(wide, axis=1, keepdims=True)
    centered = wide - average
    inverse = lax.rsqrt(jnp.mean(centered * centered, axis=1, keepdims=True) + 1e-06)
    scaled = centered * inverse
    normed = (scaled * ln_gain + ln_bias).astype(jnp.bfloat16)
    preact = jnp.dot(normed, w_up, preferred_element_type=jnp.float32) + b_up
    hidden = gelu_fn(preact).astype(jnp.bfloat16)
    hidden_other = lax.ppermute(hidden, "ylo", [(0, 1), (1, 0)])
    bias_row = lax.dynamic_update_slice_in_dim(
        jnp.zeros((WIDE,), jnp.float32), b_down, col0, 0
    )
    part = jnp.dot(hidden, w_down, preferred_element_type=jnp.float32) + bias_row
    parts = lax.all_to_all(
        part.astype(jnp.bfloat16), TENS, split_axis=0, concat_axis=0, tiled=True
    )
    mixed = jnp.sum(parts.reshape(8, IMG, WIDE).astype(jnp.float32), axis=0)
    own = lax.dynamic_slice_in_dim(both, row0, IMG, 0).astype(jnp.float32)
    summed = own + mixed
    img_norm = jnp.sqrt(jnp.sum(summed * summed, axis=1, keepdims=True) + 1e-06)
    img_unit = summed / img_norm
    img_ids = lax.dynamic_slice_in_dim(image_ids, row0, IMG, 0)
    img_send = jnp.concatenate([img_unit.astype(jnp.bfloat16), id_columns(img_ids)], axis=1)
    img_all = lax.all_gather(img_send, RING, axis=0, tiled=True)

    temper = logit_scale[0]
    offset = logit_bias[0]
    factor = loss_scale[0] / batch
    txt_full = txt_all[:, :WIDE]
    scores = lax.dot_general(
        img_all[:, :WIDE], txt_full, (((1,), (1,)), ((), ())), preferred_element_type=jnp.float32
    )
    positive = read_ids(img_all)[:, None] == read_ids(txt_all)[None, :]
    signs = jnp.where(positive, 1.0, -1.0).astype(jnp.float32)
    margin = -signs * (temper * scores + offset)
    loss_part = jnp.sum(jnp.sum(jax.nn.softplus(margin), axis=0).reshape(8, LANES), axis=0)
    weights = (-signs * temper * factor * jax.nn.sigmoid(margin)).astype(jnp.bfloat16)
    unit_part = jnp.dot(weights, txt_full, preferred_element_type=jnp.float32)
    unit_parts = lax.all_to_all(
        unit_part.astype(jnp.bfloat16), RING, split_axis=0, concat_axis=0, tiled=True
    )
    grad_unit = jnp.sum(unit_parts.reshape(16, IMG, WIDE).astype(jnp.float32), axis=0)
    tangent = jnp.sum(img_unit * grad_unit, axis=1, keepdims=True)
    grad_low = ((grad_unit - img_unit * tangent) / img_norm).astype(jnp.bfloat16)
    loss_block = jnp.pad(to_digits(loss_part), ((0, 0), (0, EXTRA - LANES)))
    grad_all = lax.all_gather(
        jnp.concatenate([grad_low, loss_block], axis=1), RING, axis=0, tiled=True
    )
    ylo = lax.axis_index("ylo")
    grad_full = lax.dynamic_slice(grad_all, (ylo * ROWS, 0), (ROWS, WIDE))
    grad_other = lax.dynamic_slice(grad_all, ((1 - ylo) * ROWS, 0), (ROWS, WIDE))
    down_part = lax.dot_general(
        jnp.concatenate([grad_full, grad_other], axis=0),
        jnp.concatenate([hidden, hidden_other], axis=0),
        (((0,), (0,)), ((), ())),
        preferred_element_type=jnp.float32,
    )
    down_part = lax.dynamic_index_in_dim(
        down_part.reshape(4, 8, 2, 24, 384), ylo, 2, keepdims=False
    ).astype(jnp.bfloat16)
    ring_digits = jnp.sum(
        grad_all.reshape(16, IMG, WIDE + EXTRA)[:, :, WIDE:].astype(jnp.float32), axis=0
    ).astype(jnp.bfloat16)
    down_send = jnp.concatenate(
        [
            down_part.reshape(4, 192, 384),
            jnp.broadcast_to(jnp.pad(ring_digits, ((0, 0), (0, 256))), (4, IMG, 384)),
        ],
        axis=1,
    ).reshape(832, 384)
    down_x = lax.psum_scatter(down_send, "x", scatter_dimension=0, tiled=True)

    grad_hidden = lax.dot_general(
        grad_full, w_down, (((1,), (1,)), ((), ())), preferred_element_type=jnp.float32
    )
    grad_pre = jax.vjp(gelu_fn, preact)[1](grad_hidden)[0].astype(jnp.bfloat16)
    normed_part = lax.dot_general(
        w_up, grad_pre, (((1,), (1,)), ((), ())), preferred_element_type=jnp.float32
    )
    gained = normed_part * ln_gain[:, None]
    sum_h = jnp.sum(gained, axis=0)
    sum_hs = jnp.sum(gained * scaled.T, axis=0)
    stats = jnp.pad(
        pieces(jnp.stack([sum_h, sum_hs]), 2).reshape(4, ROWS), ((0, 12), (0, 0))
    )
    norm_send = jnp.concatenate(
        [
            normed_part.astype(jnp.bfloat16).reshape(8, SLICE, ROWS),
            jnp.broadcast_to(stats, (8, 16, ROWS)),
        ],
        axis=1,
    )
    norm_parts = lax.all_to_all(norm_send, TENS, split_axis=0, concat_axis=0, tiled=True)
    norm_sum = jnp.sum(norm_parts.astype(jnp.float32), axis=0)
    centre = (norm_sum[SLICE] + norm_sum[SLICE + 2]) / WIDE
    along = (norm_sum[SLICE + 1] + norm_sum[SLICE + 3]) / WIDE
    gain_own = lax.dynamic_slice_in_dim(ln_gain, col0, SLICE, 0)
    scaled_own = (pooled.astype(jnp.float32) - average) * inverse
    h_own = norm_sum[:SLICE].T * gain_own[None, :]
    grad_own = lax.dynamic_slice_in_dim(grad_full, col0, SLICE, 1).astype(jnp.float32)
    grad_input = inverse * (h_own - centre[:, None] - scaled_own * along[:, None])
    grad_pooled = (grad_own + grad_input).astype(jnp.bfloat16)

    loss_tail = jnp.pad(
        pieces(from_digits(down_x[192:, :LANES]), 3), ((0, 5), (0, 384 - LANES))
    )
    last_send = jnp.concatenate(
        [down_x[:192].reshape(8, 24, 384), jnp.broadcast_to(loss_tail, (8, 8, 384))], axis=1
    )
    last = lax.all_to_all(last_send, "z", split_axis=0, concat_axis=0, tiled=True)
    last_sum = jnp.sum(last.astype(jnp.float32), axis=0)
    grad_down = last_sum[:24].T
    loss = (jnp.sum(last_sum[24:27, :LANES]) / batch).reshape(1)
    return (loss, grad_pooled, grad_down)


def solution(mesh):
    inner = Mesh(mesh.devices.reshape(4, 8, 2, 4, 2), DATA + TENS)
    placed = (
        P(DATA, TENS),
        P(),
        P(),
        P(None, TENS),
        P(TENS),
        P(TENS, None),
        P(TENS),
        P(DATA, TENS),
        P(DATA),
        P(DATA),
        P(),
        P(),
        P(),
    )
    return jax.shard_map(
        shards,
        mesh=inner,
        in_specs=placed,
        out_specs=(P(), P(DATA, TENS), P(TENS, DATA)),
        check_vma=False,
    )
```

```python
import jax
import jax.numpy as jnp
from jax import lax
from jax.experimental import pallas as pl
from jax.experimental.pallas import tpu as pltpu
from jax.sharding import Mesh, PartitionSpec as P

ROWS = 128
WIDE = 1536
SLICE = 192
EXTRA = 128
IMG = 16
DATA = ("x", "z", "ylo")
TENS = ("yhi", "core")
RING = ("ylo", "yhi", "core")


def gelu_fn(values):
    return jax.nn.gelu(values, approximate=True)


def id_columns(ids, start):
    lanes = lax.broadcasted_iota(jnp.int32, (IMG, ROWS), 1)
    rows = lax.broadcasted_iota(jnp.int32, (IMG, ROWS), 0)
    own = jnp.sum(
        jnp.where(lanes == rows + start, ids[None, :], 0).astype(jnp.float32), axis=1, keepdims=True
    )
    high = jnp.floor(own / 128.0)
    low = own - 128.0 * high
    place = lax.broadcasted_iota(jnp.int32, (IMG, EXTRA), 1)
    return jnp.where(place == 0, high, jnp.where(place == 1, low, 0.0)).astype(jnp.bfloat16)


def pieces(values, count):
    parts = []
    for _ in range(count):
        part = lax.reduce_precision(values, 8, 7)
        parts.append(part.astype(jnp.bfloat16))
        values = values - part
    return jnp.stack(parts)


def spread(block, axis, count):
    send = jnp.broadcast_to(block[None], (count,) + block.shape)
    return lax.all_to_all(send, axis, split_axis=0, concat_axis=0, tiled=True).reshape(
        count * block.shape[0], block.shape[1]
    )


VMEM = pl.BlockSpec(memory_space=pltpu.VMEM)
SMEM = pl.BlockSpec(memory_space=pltpu.SMEM)


def call(kernel, outs, n_smem, flops, moved, *args):
    return pl.pallas_call(
        kernel,
        out_shape=[jax.ShapeDtypeStruct(shape, kind) for shape, kind in outs],
        in_specs=[SMEM] * n_smem + [VMEM] * (len(args) - n_smem),
        out_specs=[VMEM] * len(outs),
        compiler_params=pltpu.CompilerParams(vmem_limit_bytes=32 * 2**20),
        cost_estimate=pl.CostEstimate(flops=flops, bytes_accessed=moved, transcendentals=0),
    )(*args)


def split_two(values):
    first = values.astype(jnp.bfloat16).astype(jnp.float32)
    return first, values - first


def pair_kernel(which_ref, scalar_ref, img_ref, txt_ref, out_ref, loss_ref):
    img = img_ref[:, which_ref[0]].reshape(ROWS, WIDE + EXTRA)
    txt = txt_ref[:, :WIDE]
    across = (((1,), (1,)), ((), ()))
    scores = lax.dot_general(img[:, :WIDE], txt, across, preferred_element_type=jnp.float32)
    place = lax.broadcasted_iota(jnp.int32, (8, EXTRA), 1)
    pick = jnp.where(place == 0, 128.0, jnp.where(place == 1, 1.0, 0.0))
    txt_ids = lax.dot_general(
        pick.astype(jnp.bfloat16), txt_ref[:, WIDE:], across, preferred_element_type=jnp.float32
    )[:1]
    img_ids = jnp.sum(img[:, WIDE:].astype(jnp.float32) * pick[:1], axis=1, keepdims=True)
    logits = scalar_ref[0] * scores + scalar_ref[1]
    positive = img_ids == txt_ids
    margin = jnp.where(positive, -logits, logits)
    shrunk = jnp.exp(-jnp.abs(margin))
    losses = jnp.maximum(margin, 0.0) + jnp.log1p(shrunk)
    sigmoid = jnp.where(margin >= 0.0, 1.0, shrunk) / (1.0 + shrunk)
    scale = scalar_ref[2]
    weights = (jnp.where(positive, -scale, scale) * sigmoid).astype(jnp.bfloat16)
    out_ref[...] = jnp.dot(weights, txt, preferred_element_type=jnp.float32).astype(out_ref.dtype)
    folded = losses[:, :128] + losses[:, 128:256] + losses[:, 256:384] + losses[:, 384:]
    loss_ref[...] = jnp.sum(folded.reshape(16, 8, 128), axis=0)


def pair_rows(which, scalars, img_all, txt_all, kind):
    return call(
        pair_kernel,
        [((ROWS, WIDE), kind), ((8, 128), jnp.float32)],
        2,
        4 * ROWS * 512 * WIDE,
        3000000,
        which.reshape(1).astype(jnp.int32),
        scalars,
        img_all.reshape(8, 2, IMG, WIDE + EXTRA),
        txt_all,
    )


def gelu_slope(values):
    root = 0.7978845608028654
    inner = jnp.tanh(root * (values + 0.044715 * (values * values * values)))
    return 0.5 * (1.0 + inner) + 0.5 * values * (1.0 - inner * inner) * root * (
        1.0 + 3.0 * 0.044715 * (values * values)
    )


def back_kernel(
    where_ref, grad_ref, down_ref, pre_ref, up_ref, gain_ref, gs_ref, send_ref, own_ref, sum_ref, hold_ref
):
    across = (((1,), (1,)), ((), ()))
    core = where_ref[1]
    grad = grad_ref[where_ref[0]][:, :WIDE]
    grad_hidden = lax.dot_general(grad, down_ref[...], across, preferred_element_type=jnp.float32)
    grad_pre = (grad_hidden * gelu_slope(pre_ref[...])).astype(jnp.bfloat16)
    part = lax.dot_general(up_ref[...], grad_pre, across, preferred_element_type=jnp.float32)
    hold_ref[...] = part.reshape(4, 2, SLICE, ROWS)
    sum_h = jnp.sum(part * gain_ref[...], axis=0, keepdims=True)
    sum_hs = jnp.sum(part * gs_ref[...], axis=0, keepdims=True)
    send_ref[: 4 * SLICE] = hold_ref[:, 1 - core].reshape(4 * SLICE, ROWS).astype(jnp.bfloat16)
    own_ref[...] = hold_ref[:, core]
    write_sums(send_ref, 4 * SLICE, sum_h, sum_hs)
    sum_ref[...] = jnp.concatenate([sum_h, sum_hs, jnp.zeros((6, ROWS), jnp.float32)], axis=0)


def write_sums(ref, start, sum_h, sum_hs):
    h_hi, h_lo = split_two(sum_h)
    s_hi, s_lo = split_two(sum_hs)
    ref[start:] = jnp.concatenate(
        [h_hi, s_hi, h_lo, s_lo, jnp.zeros((12, ROWS), jnp.float32)], axis=0
    ).astype(jnp.bfloat16)


def read_sums(ref, start):
    block = ref[start:].astype(jnp.float32)
    return block[0:1] + block[2:3], block[1:2] + block[3:4]


def back_rows(where, grad_all, w_down, preact, w_up, gain_t, gs_t):
    return pl.pallas_call(
        back_kernel,
        out_shape=[
            jax.ShapeDtypeStruct((4 * SLICE + 16, ROWS), jnp.bfloat16),
            jax.ShapeDtypeStruct((4, SLICE, ROWS), jnp.float32),
            jax.ShapeDtypeStruct((8, ROWS), jnp.float32),
        ],
        in_specs=[SMEM] + [VMEM] * 6,
        out_specs=[VMEM] * 3,
        scratch_shapes=[pltpu.VMEM((4, 2, SLICE, ROWS), jnp.float32)],
        compiler_params=pltpu.CompilerParams(vmem_limit_bytes=32 * 2**20),
        cost_estimate=pl.CostEstimate(
            flops=4 * ROWS * 384 * WIDE, bytes_accessed=4000000, transcendentals=0
        ),
    )(where, grad_all.reshape(2, ROWS, WIDE + EXTRA), w_down, preact, w_up, gain_t, gs_t)


def chip_kernel(where_ref, own_ref, sums_ref, got_ref, one_ref, two_ref, three_ref, keep_ref, all_ref, hold_ref):
    yhi = where_ref[2]
    hold_ref[...] = own_ref[...] + got_ref[: 4 * SLICE].astype(jnp.float32).reshape(4, SLICE, ROWS)
    got_h, got_hs = read_sums(got_ref, 4 * SLICE)
    sum_h = sums_ref[0:1] + got_h
    sum_hs = sums_ref[1:2] + got_hs
    for step, ref in enumerate((one_ref, two_ref, three_ref), 1):
        ref[:SLICE] = hold_ref[lax.rem(yhi + step, 4)].astype(jnp.bfloat16)
        write_sums(ref, SLICE, sum_h, sum_hs)
    keep_ref[...] = hold_ref[yhi]
    all_ref[...] = jnp.concatenate([sum_h, sum_hs, jnp.zeros((6, ROWS), jnp.float32)], axis=0)


def chip_rows(where, own_blocks, own_sums, got):
    return pl.pallas_call(
        chip_kernel,
        out_shape=[jax.ShapeDtypeStruct((SLICE + 16, ROWS), jnp.bfloat16)] * 3
        + [
            jax.ShapeDtypeStruct((SLICE, ROWS), jnp.float32),
            jax.ShapeDtypeStruct((8, ROWS), jnp.float32),
        ],
        in_specs=[SMEM] + [VMEM] * 3,
        out_specs=[VMEM] * 5,
        scratch_shapes=[pltpu.VMEM((4, SLICE, ROWS), jnp.float32)],
        compiler_params=pltpu.CompilerParams(vmem_limit_bytes=16 * 2**20),
        cost_estimate=pl.CostEstimate(flops=1000000, bytes_accessed=1000000, transcendentals=0),
    )(where, own_blocks, own_sums, got)


def last_kernel(
    keep_ref, all_ref, one_ref, two_ref, three_ref, inv_ref, invgain_ref, invscaled_ref, grad_ref, out_ref
):
    total = keep_ref[...]
    sum_h = all_ref[0:1]
    sum_hs = all_ref[1:2]
    for ref in (one_ref, two_ref, three_ref):
        total = total + ref[:SLICE].astype(jnp.float32)
        got_h, got_hs = read_sums(ref, SLICE)
        sum_h = sum_h + got_h
        sum_hs = sum_hs + got_hs
    side = (
        invgain_ref[...] * total
        - inv_ref[:1] * (sum_h / WIDE)
        - invscaled_ref[...] * (sum_hs / WIDE)
    )
    out_ref[...] = (grad_ref[...].astype(jnp.float32) + side.T).astype(jnp.bfloat16)


def last_rows(keep, sums, gots, inverse_t, invgain, invscaled, grad_own):
    return call(
        last_kernel,
        [((ROWS, SLICE), jnp.bfloat16)],
        0,
        1000000,
        800000,
        keep,
        sums,
        *gots,
        inverse_t,
        invgain,
        invscaled,
        grad_own,
    )[0]


def down_kernel(ylo_ref, grad_ref, hidden_ref, out_ref):
    even = ylo_ref[0] == 0
    rows = grad_ref[:, :WIDE]
    for piece in range(3):
        part = lax.dot_general(
            rows,
            hidden_ref[:, piece * 128 : (piece + 1) * 128],
            (((0,), (0,)), ((), ())),
            preferred_element_type=jnp.float32,
        ).reshape(32, 2, 24, 128)
        out_ref[:, piece * 24 : (piece + 1) * 24, :] = jnp.where(
            even, part[:, 0], part[:, 1]
        ).astype(jnp.bfloat16)
    tail = grad_ref[:, WIDE:].astype(jnp.float32)
    total = jnp.sum(tail, axis=0, keepdims=True)
    first = total.astype(jnp.bfloat16).astype(jnp.float32)
    second = (total - first).astype(jnp.bfloat16).astype(jnp.float32)
    third = total - first - second
    place = lax.broadcasted_iota(jnp.int32, (8, 128), 0)
    block = jnp.where(
        place == 0, first, jnp.where(place == 1, second, jnp.where(place == 2, third, 0.0))
    )
    out_ref[:, 72:, :] = jnp.broadcast_to(block[None], (32, 8, 128)).astype(jnp.bfloat16)


def down_block(ylo, grad_all, hidden_pair):
    return pl.pallas_call(
        down_kernel,
        out_shape=jax.ShapeDtypeStruct((32, 80, 128), jnp.bfloat16),
        in_specs=[
            pl.BlockSpec(memory_space=pltpu.SMEM),
            pl.BlockSpec(memory_space=pltpu.VMEM),
            pl.BlockSpec(memory_space=pltpu.VMEM),
        ],
        out_specs=pl.BlockSpec(memory_space=pltpu.VMEM),
        compiler_params=pltpu.CompilerParams(vmem_limit_bytes=24 * 2**20),
        cost_estimate=pl.CostEstimate(
            flops=2 * 256 * WIDE * 384, bytes_accessed=1700000, transcendentals=0
        ),
    )(ylo.reshape(1).astype(jnp.int32), grad_all, hidden_pair)


def turn(step):
    return [(at, (at + step) % 4) for at in range(4)]


def shards(
    pooled,
    ln_gain,
    ln_bias,
    w_up,
    b_up,
    w_down,
    b_down,
    text_embed,
    image_ids,
    text_ids,
    logit_scale,
    logit_bias,
    loss_scale,
):
    tens = lax.axis_index(TENS)
    row0 = tens * IMG
    col0 = tens * SLICE
    batch = ROWS * 64

    both = lax.all_gather(
        jnp.concatenate([pooled, text_embed], axis=0), TENS, axis=1, tiled=True
    )
    txt_rows = lax.dynamic_slice_in_dim(both, ROWS + row0, IMG, 0).astype(jnp.float32)
    txt_norm = jnp.sqrt(jnp.sum(txt_rows * txt_rows, axis=1, keepdims=True) + 1e-06)
    txt_low = (txt_rows / txt_norm).astype(jnp.bfloat16)
    txt_z = spread(jnp.concatenate([txt_low, id_columns(text_ids, row0)], axis=1), "z", 8)

    wide = both[:ROWS].astype(jnp.float32)
    average = jnp.mean(wide, axis=1, keepdims=True)
    centered = wide - average
    inverse = lax.rsqrt(jnp.mean(centered * centered, axis=1, keepdims=True) + 1e-06)
    scaled = centered * inverse
    normed = (scaled * ln_gain + ln_bias).astype(jnp.bfloat16)
    preact = jnp.dot(normed, w_up, preferred_element_type=jnp.float32) + b_up
    hidden = gelu_fn(preact).astype(jnp.bfloat16)
    hidden_other = lax.ppermute(hidden, "ylo", [(0, 1), (1, 0)])
    ylo = lax.axis_index("ylo")
    hidden_pair = jnp.concatenate(
        [jnp.where(ylo == 0, hidden, hidden_other), jnp.where(ylo == 0, hidden_other, hidden)],
        axis=0,
    )
    bias_row = lax.dynamic_update_slice_in_dim(
        jnp.zeros((WIDE,), jnp.float32), b_down, col0, 0
    )
    part = jnp.dot(hidden, w_down, preferred_element_type=jnp.float32) + bias_row
    core = lax.axis_index("core")
    yhi = lax.axis_index("yhi")
    part = part.reshape(4, 2, IMG, WIDE)
    core_got = lax.ppermute(
        lax.dynamic_index_in_dim(part, 1 - core, 1, keepdims=False).astype(jnp.bfloat16),
        "core",
        [(0, 1), (1, 0)],
    )
    chip = lax.dynamic_index_in_dim(part, core, 1, keepdims=False) + core_got.astype(jnp.float32)
    mixed = lax.dynamic_index_in_dim(chip, yhi, 0, keepdims=False)
    for step in range(1, 4):
        block = lax.dynamic_index_in_dim(chip, (yhi + step) % 4, 0, keepdims=False)
        got = lax.ppermute(block.astype(jnp.bfloat16), "yhi", turn(step))
        mixed = mixed + got.astype(jnp.float32)
    own = lax.dynamic_slice_in_dim(both, row0, IMG, 0).astype(jnp.float32)
    summed = own + mixed
    img_norm = jnp.sqrt(jnp.sum(summed * summed, axis=1, keepdims=True) + 1e-06)
    img_unit = summed / img_norm
    txt_all = spread(txt_z, "x", 4)
    img_send = jnp.concatenate(
        [img_unit.astype(jnp.bfloat16), id_columns(image_ids, row0)], axis=1
    )
    img_all = lax.all_gather(img_send, RING, axis=0, tiled=True)

    temper = logit_scale[0]
    offset = logit_bias[0]
    factor = loss_scale[0] / batch
    scalars = jnp.stack([temper, offset, temper * factor])
    other_part, other_loss = pair_rows(1 - core, scalars, img_all, txt_all, jnp.bfloat16)
    from_other = lax.ppermute(other_part, "core", [(0, 1), (1, 0)])
    own_part, own_loss = pair_rows(core, scalars, img_all, txt_all, jnp.float32)
    loss_part = jnp.sum(other_loss + own_loss, axis=0)
    chip_part = (own_part + from_other.astype(jnp.float32)).astype(jnp.bfloat16)
    unit_parts = lax.all_to_all(
        chip_part, ("ylo", "yhi"), split_axis=0, concat_axis=0, tiled=True
    )
    grad_unit = jnp.sum(unit_parts.reshape(8, IMG, WIDE).astype(jnp.float32), axis=0)
    tangent = jnp.sum(img_unit * grad_unit, axis=1, keepdims=True)
    grad_low = ((grad_unit - img_unit * tangent) / img_norm).astype(jnp.bfloat16)
    loss_block = jnp.pad(pieces(loss_part, 3), ((0, IMG - 3), (0, 0)))
    grad_all = lax.all_gather(
        jnp.concatenate([grad_low, loss_block], axis=1), RING, axis=0, tiled=True
    )
    down_send = down_block(ylo, grad_all, hidden_pair)
    down_got = lax.all_to_all(down_send, ("x", "z"), split_axis=0, concat_axis=0, tiled=True)

    where = jnp.stack([ylo, core, yhi]).astype(jnp.int32)
    gain_t = jnp.broadcast_to(ln_gain[:, None], (WIDE, ROWS))
    send, own_blocks, own_sums = back_rows(
        where, grad_all, w_down, preact, w_up, gain_t, gain_t * scaled.T
    )
    got = lax.ppermute(send, "core", [(0, 1), (1, 0)])
    sends = chip_rows(where, own_blocks, own_sums, got)
    gots = [lax.ppermute(sends[step - 1], "yhi", turn(step)) for step in range(1, 4)]
    gain_own = lax.dynamic_slice_in_dim(ln_gain, col0, SLICE, 0)
    scaled_own = ((pooled.astype(jnp.float32) - average) * inverse).T
    inverse_t = jnp.broadcast_to(inverse.reshape(1, ROWS), (8, ROWS))
    grad_own = lax.dynamic_slice(grad_all, (ylo * ROWS, col0), (ROWS, SLICE))
    grad_pooled = last_rows(
        sends[3], sends[4], gots, inverse_t, inverse_t[:1] * gain_own[:, None],
        inverse_t[:1] * scaled_own, grad_own,
    )

    down_sum = jnp.sum(down_got.astype(jnp.float32), axis=0)
    grad_down = down_sum[:72].reshape(3, 24, 128).transpose(0, 2, 1).reshape(384, 24)
    loss = (jnp.sum(down_sum[72:75]) / batch).reshape(1)
    return (loss, grad_pooled, grad_down)


def solution(mesh):
    inner = Mesh(mesh.devices.reshape(4, 8, 2, 4, 2), DATA + TENS)
    placed = (
        P(DATA, TENS),
        P(),
        P(),
        P(None, TENS),
        P(TENS),
        P(TENS, None),
        P(TENS),
        P(DATA, TENS),
        P(DATA),
        P(DATA),
        P(),
        P(),
        P(),
    )
    return jax.shard_map(
        shards,
        mesh=inner,
        in_specs=placed,
        out_specs=(P(), P(DATA, TENS), P(TENS, DATA)),
        check_vma=False,
    )
```

```python
import jax
import jax.numpy as jnp
from jax import lax
from jax.experimental import pallas as pl
from jax.experimental.pallas import tpu as pltpu
from jax.sharding import Mesh, PartitionSpec as P

ROWS = 128
WIDE = 1536
SLICE = 192
EXTRA = 128
IMG = 16
BATCH = 8192
DATA = ("x", "z", "ylo")
TENS = ("yhi", "core")
RING = ("ylo", "yhi", "core")


def gelu_fn(values):
    return jax.nn.gelu(values, approximate=True)


def id_columns(ids, start):
    lanes = lax.broadcasted_iota(jnp.int32, (IMG, ROWS), 1)
    rows = lax.broadcasted_iota(jnp.int32, (IMG, ROWS), 0)
    own = jnp.sum(
        jnp.where(lanes == rows + start, ids[None, :], 0).astype(jnp.float32), axis=1, keepdims=True
    )
    high = jnp.floor(own / 128.0)
    low = own - 128.0 * high
    place = lax.broadcasted_iota(jnp.int32, (IMG, EXTRA), 1)
    return jnp.where(place == 0, high, jnp.where(place == 1, low, 0.0)).astype(jnp.bfloat16)


def pieces(values, count):
    parts = []
    for _ in range(count):
        part = lax.reduce_precision(values, 8, 7)
        parts.append(part.astype(jnp.bfloat16))
        values = values - part
    return jnp.stack(parts)


def spread(block, axis, count):
    send = jnp.broadcast_to(block[None], (count,) + block.shape)
    return lax.all_to_all(send, axis, split_axis=0, concat_axis=0, tiled=True).reshape(
        count * block.shape[0], block.shape[1]
    )


VMEM = pl.BlockSpec(memory_space=pltpu.VMEM)
SMEM = pl.BlockSpec(memory_space=pltpu.SMEM)


def call(kernel, outs, n_smem, flops, moved, *args):
    return pl.pallas_call(
        kernel,
        out_shape=[jax.ShapeDtypeStruct(shape, kind) for shape, kind in outs],
        in_specs=[SMEM] * n_smem + [VMEM] * (len(args) - n_smem),
        out_specs=[VMEM] * len(outs),
        compiler_params=pltpu.CompilerParams(vmem_limit_bytes=32 * 2**20),
        cost_estimate=pl.CostEstimate(flops=flops, bytes_accessed=moved, transcendentals=0),
    )(*args)


def split_two(values):
    first = values.astype(jnp.bfloat16).astype(jnp.float32)
    return first, values - first


def pair_kernel(which_ref, scalar_ref, img_ref, txt_ref, *refs):
    out_ref, loss_ref = refs[-2:]
    img = img_ref[:, which_ref[0]].reshape(ROWS, WIDE + EXTRA)
    txt = txt_ref[:, :WIDE]
    across = (((1,), (1,)), ((), ()))
    scores = lax.dot_general(img[:, :WIDE], txt, across, preferred_element_type=jnp.float32)
    place = lax.broadcasted_iota(jnp.int32, (8, EXTRA), 1)
    pick = jnp.where(place == 0, 128.0, jnp.where(place == 1, 1.0, 0.0))
    txt_ids = lax.dot_general(
        pick.astype(jnp.bfloat16), txt_ref[:, WIDE:], across, preferred_element_type=jnp.float32
    )[:1]
    img_ids = jnp.sum(img[:, WIDE:].astype(jnp.float32) * pick[:1], axis=1, keepdims=True)
    logits = scalar_ref[0] * scores + scalar_ref[1]
    positive = img_ids == txt_ids
    margin = jnp.where(positive, -logits, logits)
    shrunk = jnp.exp(-jnp.abs(margin))
    losses = jnp.maximum(margin, 0.0) + jnp.log1p(shrunk)
    sigmoid = jnp.where(margin >= 0.0, 1.0, shrunk) / (1.0 + shrunk)
    scale = scalar_ref[2]
    weights = (jnp.where(positive, -scale, scale) * sigmoid).astype(jnp.bfloat16)
    part = jnp.dot(weights, txt, preferred_element_type=jnp.float32)
    if len(refs) == 3:
        part = part + refs[0][...].astype(jnp.float32)
    out_ref[...] = part.astype(jnp.bfloat16)
    folded = losses[:, :128] + losses[:, 128:256] + losses[:, 256:384] + losses[:, 384:]
    loss_ref[...] = jnp.sum(folded.reshape(16, 8, 128), axis=0)


def pair_rows(which, scalars, img_all, txt_all, *added):
    return call(
        pair_kernel,
        [((ROWS, WIDE), jnp.bfloat16), ((8, 128), jnp.float32)],
        2,
        4 * ROWS * 512 * WIDE,
        3000000,
        which.reshape(1).astype(jnp.int32),
        scalars,
        img_all.reshape(8, 2, IMG, WIDE + EXTRA),
        txt_all,
        *added,
    )


def gelu_slope(values):
    root = 0.7978845608028654
    inner = jnp.tanh(root * (values + 0.044715 * (values * values * values)))
    return 0.5 * (1.0 + inner) + 0.5 * values * (1.0 - inner * inner) * root * (
        1.0 + 3.0 * 0.044715 * (values * values)
    )


def back_kernel(
    where_ref, grad_ref, down_ref, pre_ref, up_ref, gain_ref, gs_ref, send_ref, own_ref, sum_ref, hold_ref
):
    across = (((1,), (1,)), ((), ()))
    core = where_ref[1]
    grad = grad_ref[where_ref[0]][:, :WIDE]
    grad_hidden = lax.dot_general(grad, down_ref[...], across, preferred_element_type=jnp.float32)
    grad_pre = (grad_hidden * gelu_slope(pre_ref[...])).astype(jnp.bfloat16)
    part = lax.dot_general(up_ref[...], grad_pre, across, preferred_element_type=jnp.float32)
    hold_ref[...] = part.reshape(4, 2, SLICE, ROWS)
    sum_h = jnp.sum(part * gain_ref[...], axis=0, keepdims=True)
    sum_hs = jnp.sum(part * gs_ref[...], axis=0, keepdims=True)
    send_ref[: 4 * SLICE] = hold_ref[:, 1 - core].reshape(4 * SLICE, ROWS).astype(jnp.bfloat16)
    own_ref[...] = hold_ref[:, core]
    write_sums(send_ref, 4 * SLICE, sum_h, sum_hs)
    sum_ref[...] = jnp.concatenate([sum_h, sum_hs, jnp.zeros((6, ROWS), jnp.float32)], axis=0)


def write_sums(ref, start, sum_h, sum_hs):
    h_hi, h_lo = split_two(sum_h)
    s_hi, s_lo = split_two(sum_hs)
    ref[start:] = jnp.concatenate(
        [h_hi, s_hi, h_lo, s_lo, jnp.zeros((12, ROWS), jnp.float32)], axis=0
    ).astype(jnp.bfloat16)


def read_sums(ref, start):
    block = ref[start:].astype(jnp.float32)
    return block[0:1] + block[2:3], block[1:2] + block[3:4]


def back_rows(where, grad_all, w_down, preact, w_up, gain_t, gs_t):
    return pl.pallas_call(
        back_kernel,
        out_shape=[
            jax.ShapeDtypeStruct((4 * SLICE + 16, ROWS), jnp.bfloat16),
            jax.ShapeDtypeStruct((4, SLICE, ROWS), jnp.float32),
            jax.ShapeDtypeStruct((8, ROWS), jnp.float32),
        ],
        in_specs=[SMEM] + [VMEM] * 6,
        out_specs=[VMEM] * 3,
        scratch_shapes=[pltpu.VMEM((4, 2, SLICE, ROWS), jnp.float32)],
        compiler_params=pltpu.CompilerParams(vmem_limit_bytes=32 * 2**20),
        cost_estimate=pl.CostEstimate(
            flops=4 * ROWS * 384 * WIDE, bytes_accessed=4000000, transcendentals=0
        ),
    )(where, grad_all.reshape(2, ROWS, WIDE + EXTRA), w_down, preact, w_up, gain_t, gs_t)


def chip_kernel(where_ref, own_ref, sums_ref, got_ref, one_ref, two_ref, three_ref, keep_ref, all_ref, hold_ref):
    yhi = where_ref[2]
    hold_ref[...] = own_ref[...] + got_ref[: 4 * SLICE].astype(jnp.float32).reshape(4, SLICE, ROWS)
    got_h, got_hs = read_sums(got_ref, 4 * SLICE)
    sum_h = sums_ref[0:1] + got_h
    sum_hs = sums_ref[1:2] + got_hs
    for step, ref in enumerate((one_ref, two_ref, three_ref), 1):
        ref[:SLICE] = hold_ref[lax.rem(yhi + step, 4)].astype(jnp.bfloat16)
        write_sums(ref, SLICE, sum_h, sum_hs)
    keep_ref[...] = hold_ref[yhi]
    all_ref[...] = jnp.concatenate([sum_h, sum_hs, jnp.zeros((6, ROWS), jnp.float32)], axis=0)


def chip_rows(where, own_blocks, own_sums, got):
    return pl.pallas_call(
        chip_kernel,
        out_shape=[jax.ShapeDtypeStruct((SLICE + 16, ROWS), jnp.bfloat16)] * 3
        + [
            jax.ShapeDtypeStruct((SLICE, ROWS), jnp.float32),
            jax.ShapeDtypeStruct((8, ROWS), jnp.float32),
        ],
        in_specs=[SMEM] + [VMEM] * 3,
        out_specs=[VMEM] * 5,
        scratch_shapes=[pltpu.VMEM((4, SLICE, ROWS), jnp.float32)],
        compiler_params=pltpu.CompilerParams(vmem_limit_bytes=16 * 2**20),
        cost_estimate=pl.CostEstimate(flops=1000000, bytes_accessed=1000000, transcendentals=0),
    )(where, own_blocks, own_sums, got)


def last_kernel(
    keep_ref, all_ref, one_ref, two_ref, three_ref, inv_ref, invgain_ref, invscaled_ref, grad_ref, got_ref, out_ref, down_ref, loss_ref
):
    total = keep_ref[...]
    sum_h = all_ref[0:1]
    sum_hs = all_ref[1:2]
    for ref in (one_ref, two_ref, three_ref):
        total = total + ref[:SLICE].astype(jnp.float32)
        got_h, got_hs = read_sums(ref, SLICE)
        sum_h = sum_h + got_h
        sum_hs = sum_hs + got_hs
    side = (
        invgain_ref[...] * total
        - inv_ref[:1] * (sum_h / WIDE)
        - invscaled_ref[...] * (sum_hs / WIDE)
    )
    out_ref[...] = (grad_ref[...].astype(jnp.float32) + side.T).astype(jnp.bfloat16)
    summed = jnp.sum(got_ref[...].astype(jnp.float32), axis=0)
    for piece in range(3):
        down_ref[piece * 128 : (piece + 1) * 128] = summed[piece * 24 : (piece + 1) * 24].T
    tail = jnp.sum(summed[72:], axis=1, keepdims=True)
    loss_ref[...] = jnp.sum(tail, axis=0, keepdims=True) / BATCH


def last_rows(keep, sums, gots, inverse_t, invgain, invscaled, grad_own, down_got):
    return call(
        last_kernel,
        [
            ((ROWS, SLICE), jnp.bfloat16),
            ((384, 24), jnp.float32),
            ((1, 1), jnp.float32),
        ],
        0,
        1000000,
        1600000,
        keep,
        sums,
        *gots,
        inverse_t,
        invgain,
        invscaled,
        grad_own,
        down_got,
    )


def down_kernel(ylo_ref, grad_ref, hidden_ref, other_ref, out_ref):
    even = ylo_ref[0] == 0
    rows = grad_ref[:, :WIDE]
    mine = hidden_ref[...]
    other = other_ref[...]
    hidden = jnp.concatenate(
        [jnp.where(even, mine, other), jnp.where(even, other, mine)], axis=0
    )
    for piece in range(3):
        part = lax.dot_general(
            rows,
            hidden[:, piece * 128 : (piece + 1) * 128],
            (((0,), (0,)), ((), ())),
            preferred_element_type=jnp.float32,
        ).reshape(32, 2, 24, 128)
        out_ref[:, piece * 24 : (piece + 1) * 24, :] = jnp.where(
            even, part[:, 0], part[:, 1]
        ).astype(jnp.bfloat16)
    tail = grad_ref[:, WIDE:].astype(jnp.float32)
    total = jnp.sum(tail, axis=0, keepdims=True)
    first = total.astype(jnp.bfloat16).astype(jnp.float32)
    second = (total - first).astype(jnp.bfloat16).astype(jnp.float32)
    third = total - first - second
    place = lax.broadcasted_iota(jnp.int32, (8, 128), 0)
    block = jnp.where(
        place == 0, first, jnp.where(place == 1, second, jnp.where(place == 2, third, 0.0))
    )
    out_ref[:, 72:, :] = jnp.broadcast_to(block[None], (32, 8, 128)).astype(jnp.bfloat16)


def down_block(ylo, grad_all, hidden, hidden_other):
    return pl.pallas_call(
        down_kernel,
        out_shape=jax.ShapeDtypeStruct((32, 80, 128), jnp.bfloat16),
        in_specs=[
            pl.BlockSpec(memory_space=pltpu.SMEM),
            pl.BlockSpec(memory_space=pltpu.VMEM),
            pl.BlockSpec(memory_space=pltpu.VMEM),
            pl.BlockSpec(memory_space=pltpu.VMEM),
        ],
        out_specs=pl.BlockSpec(memory_space=pltpu.VMEM),
        compiler_params=pltpu.CompilerParams(vmem_limit_bytes=24 * 2**20),
        cost_estimate=pl.CostEstimate(
            flops=2 * 256 * WIDE * 384, bytes_accessed=1700000, transcendentals=0
        ),
    )(ylo.reshape(1).astype(jnp.int32), grad_all, hidden, hidden_other)


def turn(step):
    return [(at, (at + step) % 4) for at in range(4)]


def shards(
    pooled,
    ln_gain,
    ln_bias,
    w_up,
    b_up,
    w_down,
    b_down,
    text_embed,
    image_ids,
    text_ids,
    logit_scale,
    logit_bias,
    loss_scale,
):
    tens = lax.axis_index(TENS)
    row0 = tens * IMG
    col0 = tens * SLICE

    both = lax.all_gather(
        jnp.concatenate([pooled, text_embed], axis=0), TENS, axis=1, tiled=True
    )
    txt_rows = lax.dynamic_slice_in_dim(both, ROWS + row0, IMG, 0).astype(jnp.float32)
    txt_norm = jnp.sqrt(jnp.sum(txt_rows * txt_rows, axis=1, keepdims=True) + 1e-06)
    txt_low = (txt_rows / txt_norm).astype(jnp.bfloat16)
    txt_send = jnp.concatenate([txt_low, id_columns(text_ids, row0)], axis=1)

    wide = both[:ROWS].astype(jnp.float32)
    average = jnp.mean(wide, axis=1, keepdims=True)
    centered = wide - average
    inverse = lax.rsqrt(jnp.mean(centered * centered, axis=1, keepdims=True) + 1e-06)
    scaled = centered * inverse
    normed = (scaled * ln_gain + ln_bias).astype(jnp.bfloat16)
    preact = jnp.dot(normed, w_up, preferred_element_type=jnp.float32) + b_up
    hidden = gelu_fn(preact).astype(jnp.bfloat16)
    bias_row = lax.dynamic_update_slice_in_dim(
        jnp.zeros((WIDE,), jnp.float32), b_down, col0, 0
    )
    part = jnp.dot(hidden, w_down, preferred_element_type=jnp.float32) + bias_row
    core = lax.axis_index("core")
    yhi = lax.axis_index("yhi")
    part = part.reshape(4, 2, IMG, WIDE)
    part_other = lax.dynamic_index_in_dim(part, 1 - core, 1, keepdims=False).astype(jnp.bfloat16)
    part_other, txt_send = lax.optimization_barrier((part_other, txt_send))
    txt_all = spread(txt_send, ("x", "z"), 32)
    core_got = lax.ppermute(
        part_other,
        "core",
        [(0, 1), (1, 0)],
    )
    chip = lax.dynamic_index_in_dim(part, core, 1, keepdims=False) + core_got.astype(jnp.float32)
    mixed = lax.dynamic_index_in_dim(chip, yhi, 0, keepdims=False)
    for step in range(1, 4):
        block = lax.dynamic_index_in_dim(chip, (yhi + step) % 4, 0, keepdims=False)
        got = lax.ppermute(block.astype(jnp.bfloat16), "yhi", turn(step))
        mixed = mixed + got.astype(jnp.float32)
    own = lax.dynamic_slice_in_dim(both, row0, IMG, 0).astype(jnp.float32)
    summed = own + mixed
    img_norm = jnp.sqrt(jnp.sum(summed * summed, axis=1, keepdims=True) + 1e-06)
    img_unit = summed / img_norm
    img_send = jnp.concatenate(
        [img_unit.astype(jnp.bfloat16), id_columns(image_ids, row0)], axis=1
    )
    img_all = lax.all_gather(img_send, RING, axis=0, tiled=True)

    temper = logit_scale[0]
    offset = logit_bias[0]
    factor = loss_scale[0] / BATCH
    scalars = jnp.stack([temper, offset, temper * factor])
    other_part, other_loss = pair_rows(1 - core, scalars, img_all, txt_all)
    from_other = lax.ppermute(other_part, "core", [(0, 1), (1, 0)])
    chip_part, own_loss = pair_rows(core, scalars, img_all, txt_all, from_other)
    scaled_late, own_loss = lax.optimization_barrier((scaled, own_loss))
    gain_t = jnp.broadcast_to(ln_gain[:, None], (WIDE, ROWS))
    gs_t = gain_t * scaled_late.T
    hidden_late, gs_t = lax.optimization_barrier((hidden, gs_t))
    hidden_other = lax.ppermute(hidden_late, "ylo", [(0, 1), (1, 0)])
    ylo = lax.axis_index("ylo")
    unit_parts = lax.all_to_all(
        chip_part, ("ylo", "yhi"), split_axis=0, concat_axis=0, tiled=True
    )
    grad_unit = jnp.sum(unit_parts.reshape(8, IMG, WIDE).astype(jnp.float32), axis=0)
    tangent = jnp.sum(img_unit * grad_unit, axis=1, keepdims=True)
    grad_low = ((grad_unit - img_unit * tangent) / img_norm).astype(jnp.bfloat16)
    loss_part = jnp.sum(other_loss + own_loss, axis=0)
    loss_block = jnp.pad(pieces(loss_part, 3), ((0, IMG - 3), (0, 0)))
    grad_all = lax.all_gather(
        jnp.concatenate([grad_low, loss_block], axis=1), RING, axis=0, tiled=True
    )
    where = jnp.stack([ylo, core, yhi]).astype(jnp.int32)
    send, own_blocks, own_sums = back_rows(
        where, grad_all, w_down, preact, w_up, gain_t, gs_t
    )
    grad_late, send = lax.optimization_barrier((grad_all, send))
    down_send = down_block(ylo, grad_late, hidden, hidden_other)
    down_got = lax.all_to_all(down_send, ("x", "z"), split_axis=0, concat_axis=0, tiled=True)
    got = lax.ppermute(send, "core", [(0, 1), (1, 0)])
    sends = chip_rows(where, own_blocks, own_sums, got)
    gots = [lax.ppermute(sends[step - 1], "yhi", turn(step)) for step in range(1, 4)]
    gain_own = lax.dynamic_slice_in_dim(ln_gain, col0, SLICE, 0)
    scaled_own = ((pooled.astype(jnp.float32) - average) * inverse).T
    inverse_t = jnp.broadcast_to(inverse.reshape(1, ROWS), (8, ROWS))
    grad_own = lax.dynamic_slice(grad_all, (ylo * ROWS, col0), (ROWS, SLICE))
    grad_pooled, grad_down, loss = last_rows(
        sends[3], sends[4], gots, inverse_t, inverse_t[:1] * gain_own[:, None],
        inverse_t[:1] * scaled_own, grad_own, down_got,
    )
    return (loss.reshape(1), grad_pooled, grad_down)


def solution(mesh):
    inner = Mesh(mesh.devices.reshape(4, 8, 2, 4, 2), DATA + TENS)
    placed = (
        P(DATA, TENS),
        P(),
        P(),
        P(None, TENS),
        P(TENS),
        P(TENS, None),
        P(TENS),
        P(DATA, TENS),
        P(DATA),
        P(DATA),
        P(),
        P(),
        P(),
    )
    return jax.shard_map(
        shards,
        mesh=inner,
        in_specs=placed,
        out_specs=(P(), P(DATA, TENS), P(TENS, DATA)),
        check_vma=False,
    )
```

```python
import jax
import jax.numpy as jnp
from jax import lax
from jax.experimental import pallas as pl
from jax.experimental.pallas import tpu as pltpu
from jax.sharding import Mesh, PartitionSpec as P

ROWS = 128
WIDE = 1536
SLICE = 192
EXTRA = 128
IMG = 16
BATCH = 8192
DATA = ("x", "z", "ylo")
TENS = ("yhi", "core")
RING = ("ylo", "yhi", "core")


def gelu_fn(values):
    return jax.nn.gelu(values, approximate=True)


def id_columns(ids, start):
    lanes = lax.broadcasted_iota(jnp.int32, (IMG, ROWS), 1)
    rows = lax.broadcasted_iota(jnp.int32, (IMG, ROWS), 0)
    own = jnp.sum(
        jnp.where(lanes == rows + start, ids[None, :], 0).astype(jnp.float32), axis=1, keepdims=True
    )
    high = jnp.floor(own / 128.0)
    low = own - 128.0 * high
    place = lax.broadcasted_iota(jnp.int32, (IMG, EXTRA), 1)
    return jnp.where(place == 0, high, jnp.where(place == 1, low, 0.0)).astype(jnp.bfloat16)


def pieces(values, count):
    parts = []
    for _ in range(count):
        part = lax.reduce_precision(values, 8, 7)
        parts.append(part.astype(jnp.bfloat16))
        values = values - part
    return jnp.stack(parts)


VMEM = pl.BlockSpec(memory_space=pltpu.VMEM)
SMEM = pl.BlockSpec(memory_space=pltpu.SMEM)


def call(kernel, outs, n_smem, flops, moved, *args):
    return pl.pallas_call(
        kernel,
        out_shape=[jax.ShapeDtypeStruct(shape, kind) for shape, kind in outs],
        in_specs=[SMEM] * n_smem + [VMEM] * (len(args) - n_smem),
        out_specs=[VMEM] * len(outs),
        compiler_params=pltpu.CompilerParams(vmem_limit_bytes=32 * 2**20),
        cost_estimate=pl.CostEstimate(flops=flops, bytes_accessed=moved, transcendentals=0),
    )(*args)


def split_two(values):
    first = values.astype(jnp.bfloat16).astype(jnp.float32)
    return first, values - first


def pair_kernel(which_ref, scalar_ref, img_ref, txt_ref, *refs):
    out_ref, loss_ref = refs[-2:]
    img = img_ref[:, which_ref[0]].reshape(ROWS, WIDE + EXTRA)
    txt = txt_ref[:, :WIDE]
    across = (((1,), (1,)), ((), ()))
    scores = lax.dot_general(img[:, :WIDE], txt, across, preferred_element_type=jnp.float32)
    place = lax.broadcasted_iota(jnp.int32, (8, EXTRA), 1)
    pick = jnp.where(place == 0, 128.0, jnp.where(place == 1, 1.0, 0.0))
    txt_ids = lax.dot_general(
        pick.astype(jnp.bfloat16), txt_ref[:, WIDE:], across, preferred_element_type=jnp.float32
    )[:1]
    img_ids = jnp.sum(img[:, WIDE:].astype(jnp.float32) * pick[:1], axis=1, keepdims=True)
    temper = scalar_ref[:, 0:1]
    logits = temper * scores + scalar_ref[:, 1:2]
    positive = img_ids == txt_ids
    margin = jnp.where(positive, -logits, logits)
    shrunk = jnp.exp(-jnp.abs(margin))
    losses = jnp.maximum(margin, 0.0) + jnp.log1p(shrunk)
    sigmoid = jnp.where(margin >= 0.0, 1.0, shrunk) / (1.0 + shrunk)
    scale = temper * (scalar_ref[:, 2:3] / BATCH)
    weights = (jnp.where(positive, -scale, scale) * sigmoid).astype(jnp.bfloat16)
    part = jnp.dot(weights, txt, preferred_element_type=jnp.float32)
    if len(refs) == 3:
        part = part + refs[0][...].astype(jnp.float32)
    out_ref[...] = part.astype(jnp.bfloat16)
    folded = losses[:, :128] + losses[:, 128:256] + losses[:, 256:384] + losses[:, 384:]
    loss_ref[...] = jnp.sum(folded.reshape(16, 8, 128), axis=0)


def pair_rows(which, scalars, img_all, txt_all, *added):
    return call(
        pair_kernel,
        [((ROWS, WIDE), jnp.bfloat16), ((8, 128), jnp.float32)],
        1,
        4 * ROWS * 512 * WIDE,
        3000000,
        which.reshape(1).astype(jnp.int32),
        scalars,
        img_all.reshape(8, 2, IMG, WIDE + EXTRA),
        txt_all,
        *added,
    )


def gelu_slope(values):
    root = 0.7978845608028654
    inner = jnp.tanh(root * (values + 0.044715 * (values * values * values)))
    return 0.5 * (1.0 + inner) + 0.5 * values * (1.0 - inner * inner) * root * (
        1.0 + 3.0 * 0.044715 * (values * values)
    )


def back_kernel(
    where_ref, grad_ref, down_ref, pre_ref, up_ref, gain_ref, gs_ref, send_ref, own_ref, sum_ref, hold_ref
):
    across = (((1,), (1,)), ((), ()))
    core = where_ref[1]
    grad = grad_ref[where_ref[0]][:, :WIDE]
    grad_hidden = lax.dot_general(grad, down_ref[...], across, preferred_element_type=jnp.float32)
    grad_pre = (grad_hidden * gelu_slope(pre_ref[...])).astype(jnp.bfloat16)
    part = lax.dot_general(up_ref[...], grad_pre, across, preferred_element_type=jnp.float32)
    hold_ref[...] = part.reshape(4, 2, SLICE, ROWS)
    sum_h = jnp.sum(part * gain_ref[...], axis=0, keepdims=True)
    sum_hs = jnp.sum(part * gs_ref[...], axis=0, keepdims=True)
    send_ref[: 4 * SLICE] = hold_ref[:, 1 - core].reshape(4 * SLICE, ROWS).astype(jnp.bfloat16)
    own_ref[...] = hold_ref[:, core]
    write_sums(send_ref, 4 * SLICE, sum_h, sum_hs)
    sum_ref[...] = jnp.concatenate([sum_h, sum_hs, jnp.zeros((6, ROWS), jnp.float32)], axis=0)


def write_sums(ref, start, sum_h, sum_hs):
    h_hi, h_lo = split_two(sum_h)
    s_hi, s_lo = split_two(sum_hs)
    ref[start:] = jnp.concatenate(
        [h_hi, s_hi, h_lo, s_lo, jnp.zeros((12, ROWS), jnp.float32)], axis=0
    ).astype(jnp.bfloat16)


def read_sums(ref, start):
    block = ref[start:].astype(jnp.float32)
    return block[0:1] + block[2:3], block[1:2] + block[3:4]


def back_rows(where, grad_all, w_down, preact, w_up, gain_t, gs_t):
    return pl.pallas_call(
        back_kernel,
        out_shape=[
            jax.ShapeDtypeStruct((4 * SLICE + 16, ROWS), jnp.bfloat16),
            jax.ShapeDtypeStruct((4, SLICE, ROWS), jnp.float32),
            jax.ShapeDtypeStruct((8, ROWS), jnp.float32),
        ],
        in_specs=[SMEM] + [VMEM] * 6,
        out_specs=[VMEM] * 3,
        scratch_shapes=[pltpu.VMEM((4, 2, SLICE, ROWS), jnp.float32)],
        compiler_params=pltpu.CompilerParams(vmem_limit_bytes=32 * 2**20),
        cost_estimate=pl.CostEstimate(
            flops=4 * ROWS * 384 * WIDE, bytes_accessed=4000000, transcendentals=0
        ),
    )(where, grad_all.reshape(2, ROWS, WIDE + EXTRA), w_down, preact, w_up, gain_t, gs_t)


def chip_kernel(where_ref, own_ref, sums_ref, got_ref, one_ref, two_ref, three_ref, keep_ref, all_ref, hold_ref):
    yhi = where_ref[2]
    hold_ref[...] = own_ref[...] + got_ref[: 4 * SLICE].astype(jnp.float32).reshape(4, SLICE, ROWS)
    got_h, got_hs = read_sums(got_ref, 4 * SLICE)
    sum_h = sums_ref[0:1] + got_h
    sum_hs = sums_ref[1:2] + got_hs
    for step, ref in enumerate((one_ref, two_ref, three_ref), 1):
        ref[:SLICE] = hold_ref[lax.rem(yhi + step, 4)].astype(jnp.bfloat16)
        write_sums(ref, SLICE, sum_h, sum_hs)
    keep_ref[...] = hold_ref[yhi]
    all_ref[...] = jnp.concatenate([sum_h, sum_hs, jnp.zeros((6, ROWS), jnp.float32)], axis=0)


def chip_rows(where, own_blocks, own_sums, got):
    return pl.pallas_call(
        chip_kernel,
        out_shape=[jax.ShapeDtypeStruct((SLICE + 16, ROWS), jnp.bfloat16)] * 3
        + [
            jax.ShapeDtypeStruct((SLICE, ROWS), jnp.float32),
            jax.ShapeDtypeStruct((8, ROWS), jnp.float32),
        ],
        in_specs=[SMEM] + [VMEM] * 3,
        out_specs=[VMEM] * 5,
        scratch_shapes=[pltpu.VMEM((4, SLICE, ROWS), jnp.float32)],
        compiler_params=pltpu.CompilerParams(vmem_limit_bytes=16 * 2**20),
        cost_estimate=pl.CostEstimate(flops=1000000, bytes_accessed=1000000, transcendentals=0),
    )(where, own_blocks, own_sums, got)


def fore_kernel(where_ref, part_ref, got_ref, one_ref, two_ref, three_ref, keep_ref):
    core = where_ref[1]
    yhi = where_ref[2]

    def chip(at):
        return part_ref[at, core] + got_ref[at].astype(jnp.float32)

    for step, ref in enumerate((one_ref, two_ref, three_ref), 1):
        ref[...] = chip(lax.rem(yhi + step, 4)).astype(jnp.bfloat16)
    keep_ref[...] = chip(yhi)


def fore_chip(where, part, got):
    return call(
        fore_kernel,
        [((IMG, WIDE), jnp.bfloat16)] * 3 + [((IMG, WIDE), jnp.float32)],
        1,
        1000000,
        1500000,
        where,
        part,
        got,
    )


def img_kernel(keep_ref, one_ref, two_ref, three_ref, own_ref, ids_ref, send_ref, unit_ref, norm_ref):
    summed = keep_ref[...] + own_ref[...]
    for ref in (one_ref, two_ref, three_ref):
        summed = summed + ref[...].astype(jnp.float32)
    norm = jnp.sqrt(jnp.sum(summed * summed, axis=1, keepdims=True) + 1e-06)
    unit = summed / norm
    unit_ref[...] = unit
    norm_ref[...] = norm
    send_ref[:, :WIDE] = unit.astype(jnp.bfloat16)
    send_ref[:, WIDE:] = ids_ref[...]


def img_rows(keep, gots, own, ids):
    return call(
        img_kernel,
        [
            ((IMG, WIDE + EXTRA), jnp.bfloat16),
            ((IMG, WIDE), jnp.float32),
            ((IMG, 1), jnp.float32),
        ],
        0,
        200000,
        500000,
        keep,
        *gots,
        own,
        ids,
    )


def last_kernel(
    keep_ref, all_ref, one_ref, two_ref, three_ref, inv_ref, invgain_ref, invscaled_ref, grad_ref, got_ref, out_ref, down_ref, loss_ref
):
    total = keep_ref[...]
    sum_h = all_ref[0:1]
    sum_hs = all_ref[1:2]
    for ref in (one_ref, two_ref, three_ref):
        total = total + ref[:SLICE].astype(jnp.float32)
        got_h, got_hs = read_sums(ref, SLICE)
        sum_h = sum_h + got_h
        sum_hs = sum_hs + got_hs
    side = (
        invgain_ref[...] * total
        - inv_ref[:1] * (sum_h / WIDE)
        - invscaled_ref[...] * (sum_hs / WIDE)
    )
    out_ref[...] = (grad_ref[...].astype(jnp.float32) + side).astype(jnp.bfloat16)
    summed = jnp.sum(got_ref[...].astype(jnp.float32), axis=0)
    for piece in range(3):
        down_ref[:, piece * 128 : (piece + 1) * 128] = summed[piece * 24 : (piece + 1) * 24]
    tail = jnp.sum(summed[72:], axis=1, keepdims=True)
    loss_ref[...] = jnp.sum(tail, axis=0, keepdims=True) / BATCH


def last_rows(keep, sums, gots, inverse_t, invgain, invscaled, grad_own, down_got):
    return call(
        last_kernel,
        [
            ((SLICE, ROWS), jnp.bfloat16),
            ((24, 384), jnp.float32),
            ((1, 1), jnp.float32),
        ],
        0,
        1000000,
        1600000,
        keep,
        sums,
        *gots,
        inverse_t,
        invgain,
        invscaled,
        grad_own,
        down_got,
    )


def down_kernel(ylo_ref, grad_ref, hidden_ref, other_ref, out_ref):
    even = ylo_ref[0] == 0
    rows = grad_ref[:, :WIDE]
    mine = hidden_ref[...]
    other = other_ref[...]
    hidden = jnp.concatenate(
        [jnp.where(even, mine, other), jnp.where(even, other, mine)], axis=0
    )
    for piece in range(3):
        part = lax.dot_general(
            rows,
            hidden[:, piece * 128 : (piece + 1) * 128],
            (((0,), (0,)), ((), ())),
            preferred_element_type=jnp.float32,
        ).reshape(32, 2, 24, 128)
        out_ref[:, piece * 24 : (piece + 1) * 24, :] = jnp.where(
            even, part[:, 0], part[:, 1]
        ).astype(jnp.bfloat16)
    tail = grad_ref[:, WIDE:].astype(jnp.float32)
    total = jnp.sum(tail, axis=0, keepdims=True)
    first = total.astype(jnp.bfloat16).astype(jnp.float32)
    second = (total - first).astype(jnp.bfloat16).astype(jnp.float32)
    third = total - first - second
    place = lax.broadcasted_iota(jnp.int32, (8, 128), 0)
    block = jnp.where(
        place == 0, first, jnp.where(place == 1, second, jnp.where(place == 2, third, 0.0))
    )
    out_ref[:, 72:, :] = jnp.broadcast_to(block[None], (32, 8, 128)).astype(jnp.bfloat16)


def down_block(ylo, grad_all, hidden, hidden_other):
    return pl.pallas_call(
        down_kernel,
        out_shape=jax.ShapeDtypeStruct((32, 80, 128), jnp.bfloat16),
        in_specs=[
            pl.BlockSpec(memory_space=pltpu.SMEM),
            pl.BlockSpec(memory_space=pltpu.VMEM),
            pl.BlockSpec(memory_space=pltpu.VMEM),
            pl.BlockSpec(memory_space=pltpu.VMEM),
        ],
        out_specs=pl.BlockSpec(memory_space=pltpu.VMEM),
        compiler_params=pltpu.CompilerParams(vmem_limit_bytes=24 * 2**20),
        cost_estimate=pl.CostEstimate(
            flops=2 * 256 * WIDE * 384, bytes_accessed=1700000, transcendentals=0
        ),
    )(ylo.reshape(1).astype(jnp.int32), grad_all, hidden, hidden_other)


def turn(step):
    return [(at, (at + step) % 4) for at in range(4)]


def shards(
    pooled,
    ln_gain,
    ln_bias,
    w_up,
    b_up,
    w_down,
    b_down,
    text_embed,
    image_ids,
    text_ids,
    logit_scale,
    logit_bias,
    loss_scale,
):
    tens = lax.axis_index(TENS)
    row0 = tens * IMG
    col0 = tens * SLICE

    both = lax.all_gather(
        jnp.concatenate([pooled, text_embed], axis=0), TENS, axis=1, tiled=True
    )
    rows = lax.dynamic_slice_in_dim(
        both.reshape(2, ROWS, WIDE), row0, IMG, 1
    ).astype(jnp.float32)
    own, txt_rows = rows[0], rows[1]
    txt_norm = jnp.sqrt(jnp.sum(txt_rows * txt_rows, axis=1, keepdims=True) + 1e-06)
    txt_low = (txt_rows / txt_norm).astype(jnp.bfloat16)
    txt_send = jnp.concatenate([txt_low, id_columns(text_ids, row0)], axis=1)
    wide = both[:ROWS].astype(jnp.float32)
    average = jnp.mean(wide, axis=1, keepdims=True)
    centered = wide - average
    inverse = lax.rsqrt(jnp.mean(centered * centered, axis=1, keepdims=True) + 1e-06)
    scaled = centered * inverse
    normed = (scaled * ln_gain + ln_bias).astype(jnp.bfloat16)
    preact = jnp.dot(normed, w_up, preferred_element_type=jnp.float32) + b_up
    hidden = gelu_fn(preact).astype(jnp.bfloat16)
    bias_row = lax.dynamic_update_slice_in_dim(
        jnp.zeros((WIDE,), jnp.float32), b_down, col0, 0
    )
    part = jnp.dot(hidden, w_down, preferred_element_type=jnp.float32) + bias_row
    core = lax.axis_index("core")
    yhi = lax.axis_index("yhi")
    part = part.reshape(4, 2, IMG, WIDE)
    part_other = lax.dynamic_index_in_dim(part, 1 - core, 1, keepdims=False).astype(jnp.bfloat16)
    part_other, txt_send = lax.optimization_barrier((part_other, txt_send))
    core_got = lax.ppermute(
        part_other,
        "core",
        [(0, 1), (1, 0)],
    )
    txt_copies = jnp.broadcast_to(txt_send[None], (32, IMG, WIDE + EXTRA))
    txt_all = lax.all_to_all(
        txt_copies, ("x", "z"), split_axis=0, concat_axis=0, tiled=True
    ).reshape(4 * ROWS, WIDE + EXTRA)
    where = jnp.stack([lax.axis_index("ylo"), core, yhi]).astype(jnp.int32)
    sends = fore_chip(where, part, core_got)
    gots = [lax.ppermute(sends[step - 1], "yhi", turn(step)) for step in range(1, 4)]
    img_send, img_unit, img_norm = img_rows(sends[3], gots, own, id_columns(image_ids, row0))
    img_all = lax.all_gather(img_send, RING, axis=0, tiled=True)

    scalars = jnp.concatenate([logit_scale, logit_bias, loss_scale]).reshape(1, 3)
    other_part, other_loss = pair_rows(1 - core, scalars, img_all, txt_all)
    from_other = lax.ppermute(other_part, "core", [(0, 1), (1, 0)])
    chip_part, own_loss = pair_rows(core, scalars, img_all, txt_all, from_other)
    scaled_late, own_loss = lax.optimization_barrier((scaled, own_loss))
    gain_t = jnp.broadcast_to(ln_gain[:, None], (WIDE, ROWS))
    gs_t = gain_t * scaled_late.T
    hidden_late, gs_t = lax.optimization_barrier((hidden, gs_t))
    hidden_other = lax.ppermute(hidden_late, "ylo", [(0, 1), (1, 0)])
    ylo = lax.axis_index("ylo")
    unit_parts = lax.all_to_all(
        chip_part, ("ylo", "yhi"), split_axis=0, concat_axis=0, tiled=True
    )
    grad_unit = jnp.sum(unit_parts.reshape(8, IMG, WIDE).astype(jnp.float32), axis=0)
    tangent = jnp.sum(img_unit * grad_unit, axis=1, keepdims=True)
    grad_low = ((grad_unit - img_unit * tangent) / img_norm).astype(jnp.bfloat16)
    loss_part = jnp.sum(other_loss + own_loss, axis=0)
    loss_block = jnp.pad(pieces(loss_part, 3), ((0, IMG - 3), (0, 0)))
    grad_send = jnp.concatenate([grad_low, loss_block], axis=1)
    grad_send, hidden_other = lax.optimization_barrier((grad_send, hidden_other))
    grad_all = lax.all_gather(grad_send, RING, axis=0, tiled=True)
    send, own_blocks, own_sums = back_rows(
        where, grad_all, w_down, preact, w_up, gain_t, gs_t
    )
    grad_late, send = lax.optimization_barrier((grad_all, send))
    down_send = down_block(ylo, grad_late, hidden, hidden_other)
    down_got = lax.all_to_all(down_send, ("x", "z"), split_axis=0, concat_axis=0, tiled=True)
    got = lax.ppermute(send, "core", [(0, 1), (1, 0)])
    sends = chip_rows(where, own_blocks, own_sums, got)
    gots = [lax.ppermute(sends[step - 1], "yhi", turn(step)) for step in range(1, 4)]
    gain_own = lax.dynamic_slice_in_dim(ln_gain, col0, SLICE, 0)
    scaled_own = ((pooled.astype(jnp.float32) - average) * inverse).T
    inverse_t = jnp.broadcast_to(inverse.reshape(1, ROWS), (8, ROWS))
    grad_own = lax.dynamic_slice(grad_all, (ylo * ROWS, col0), (ROWS, SLICE))
    grad_pooled, grad_down, loss = last_rows(
        sends[3], sends[4], gots, inverse_t, inverse_t[:1] * gain_own[:, None],
        inverse_t[:1] * scaled_own, grad_own.T, down_got,
    )
    return (loss.reshape(1), grad_pooled.T, grad_down.T)


def solution(mesh):
    inner = Mesh(mesh.devices.reshape(4, 8, 2, 4, 2), DATA + TENS)
    placed = (
        P(DATA, TENS),
        P(),
        P(),
        P(None, TENS),
        P(TENS),
        P(TENS, None),
        P(TENS),
        P(DATA, TENS),
        P(DATA),
        P(DATA),
        P(),
        P(),
        P(),
    )
    return jax.shard_map(
        shards,
        mesh=inner,
        in_specs=placed,
        out_specs=(P(), P(DATA, TENS), P(TENS, DATA)),
        check_vma=False,
    )
```

```python
import jax
import jax.numpy as jnp
from jax import lax
from jax.experimental import pallas as pl
from jax.experimental.pallas import tpu as pltpu
from jax.sharding import Mesh, PartitionSpec as P

ROWS = 128
WIDE = 1536
SLICE = 192
EXTRA = 128
IMG = 16
BATCH = 8192
DATA = ("x", "z", "ylo")
TENS = ("yhi", "core")
RING = ("ylo", "yhi", "core")


def gelu_fn(values):
    return jax.nn.gelu(values, approximate=True)


def id_columns(ids, start):
    lanes = lax.broadcasted_iota(jnp.int32, (IMG, ROWS), 1)
    rows = lax.broadcasted_iota(jnp.int32, (IMG, ROWS), 0)
    own = jnp.sum(
        jnp.where(lanes == rows + start, ids[None, :], 0).astype(jnp.float32), axis=1, keepdims=True
    )
    high = jnp.floor(own / 128.0)
    low = own - 128.0 * high
    place = lax.broadcasted_iota(jnp.int32, (IMG, EXTRA), 1)
    return jnp.where(place == 0, high, jnp.where(place == 1, low, 0.0)).astype(jnp.bfloat16)


def pieces(values, count):
    parts = []
    for _ in range(count):
        part = lax.reduce_precision(values, 8, 7)
        parts.append(part.astype(jnp.bfloat16))
        values = values - part
    return jnp.stack(parts)


VMEM = pl.BlockSpec(memory_space=pltpu.VMEM)
SMEM = pl.BlockSpec(memory_space=pltpu.SMEM)


def call(kernel, outs, n_smem, flops, moved, *args):
    return pl.pallas_call(
        kernel,
        out_shape=[jax.ShapeDtypeStruct(shape, kind) for shape, kind in outs],
        in_specs=[SMEM] * n_smem + [VMEM] * (len(args) - n_smem),
        out_specs=[VMEM] * len(outs),
        compiler_params=pltpu.CompilerParams(vmem_limit_bytes=32 * 2**20),
        cost_estimate=pl.CostEstimate(flops=flops, bytes_accessed=moved, transcendentals=0),
    )(*args)


def split_two(values):
    first = values.astype(jnp.bfloat16).astype(jnp.float32)
    return first, values - first


def pair_kernel(which_ref, temper_ref, offset_ref, factor_ref, img_ref, txt_ref, *refs):
    out_ref, loss_ref = refs[-2:]
    img = img_ref[:, which_ref[0]].reshape(ROWS, WIDE + EXTRA)
    txt = txt_ref[:, :WIDE]
    across = (((1,), (1,)), ((), ()))
    scores = lax.dot_general(img[:, :WIDE], txt, across, preferred_element_type=jnp.float32)
    place = lax.broadcasted_iota(jnp.int32, (8, EXTRA), 1)
    pick = jnp.where(place == 0, 128.0, jnp.where(place == 1, 1.0, 0.0))
    txt_ids = lax.dot_general(
        pick.astype(jnp.bfloat16), txt_ref[:, WIDE:], across, preferred_element_type=jnp.float32
    )[:1]
    img_ids = jnp.sum(img[:, WIDE:].astype(jnp.float32) * pick[:1], axis=1, keepdims=True)
    temper = temper_ref[0]
    logits = temper * scores + offset_ref[0]
    positive = img_ids == txt_ids
    margin = jnp.where(positive, -logits, logits)
    shrunk = jnp.exp(-jnp.abs(margin))
    losses = jnp.maximum(margin, 0.0) + jnp.log1p(shrunk)
    sigmoid = jnp.where(margin >= 0.0, 1.0, shrunk) / (1.0 + shrunk)
    scale = temper * (factor_ref[0] / BATCH)
    weights = (jnp.where(positive, -scale, scale) * sigmoid).astype(jnp.bfloat16)
    part = jnp.dot(weights, txt, preferred_element_type=jnp.float32)
    if len(refs) == 3:
        part = part + refs[0][...].astype(jnp.float32)
    out_ref[...] = part.astype(jnp.bfloat16)
    folded = losses[:, :128] + losses[:, 128:256] + losses[:, 256:384] + losses[:, 384:]
    loss_ref[...] = jnp.sum(folded.reshape(16, 8, 128), axis=0)


def pair_rows(which, scalars, img_all, txt_all, *added):
    return call(
        pair_kernel,
        [((ROWS, WIDE), jnp.bfloat16), ((8, 128), jnp.float32)],
        4,
        4 * ROWS * 512 * WIDE,
        3000000,
        which.reshape(1).astype(jnp.int32),
        *scalars,
        img_all.reshape(8, 2, IMG, WIDE + EXTRA),
        txt_all,
        *added,
    )


def gelu_slope(values):
    root = 0.7978845608028654
    inner = jnp.tanh(root * (values + 0.044715 * (values * values * values)))
    return 0.5 * (1.0 + inner) + 0.5 * values * (1.0 - inner * inner) * root * (
        1.0 + 3.0 * 0.044715 * (values * values)
    )


def back_kernel(
    where_ref, grad_ref, down_ref, pre_ref, up_ref, gain_ref, gs_ref, send_ref, own_ref, sum_ref, hold_ref
):
    across = (((1,), (1,)), ((), ()))
    core = where_ref[1]
    grad = grad_ref[where_ref[0]][:, :WIDE]
    grad_hidden = lax.dot_general(grad, down_ref[...], across, preferred_element_type=jnp.float32)
    grad_pre = (grad_hidden * gelu_slope(pre_ref[...])).astype(jnp.bfloat16)
    part = lax.dot_general(up_ref[...], grad_pre, across, preferred_element_type=jnp.float32)
    hold_ref[...] = part.reshape(4, 2, SLICE, ROWS)
    sum_h = jnp.sum(part * gain_ref[...], axis=0, keepdims=True)
    sum_hs = jnp.sum(part * gs_ref[...], axis=0, keepdims=True)
    send_ref[: 4 * SLICE] = hold_ref[:, 1 - core].reshape(4 * SLICE, ROWS).astype(jnp.bfloat16)
    own_ref[...] = hold_ref[:, core]
    write_sums(send_ref, 4 * SLICE, sum_h, sum_hs)
    sum_ref[...] = jnp.concatenate([sum_h, sum_hs, jnp.zeros((6, ROWS), jnp.float32)], axis=0)


def write_sums(ref, start, sum_h, sum_hs):
    h_hi, h_lo = split_two(sum_h)
    s_hi, s_lo = split_two(sum_hs)
    ref[start:] = jnp.concatenate(
        [h_hi, s_hi, h_lo, s_lo, jnp.zeros((12, ROWS), jnp.float32)], axis=0
    ).astype(jnp.bfloat16)


def read_sums(ref, start):
    block = ref[start:].astype(jnp.float32)
    return block[0:1] + block[2:3], block[1:2] + block[3:4]


def back_rows(where, grad_all, w_down, preact, w_up, gain_t, gs_t):
    return pl.pallas_call(
        back_kernel,
        out_shape=[
            jax.ShapeDtypeStruct((4 * SLICE + 16, ROWS), jnp.bfloat16),
            jax.ShapeDtypeStruct((4, SLICE, ROWS), jnp.float32),
            jax.ShapeDtypeStruct((8, ROWS), jnp.float32),
        ],
        in_specs=[SMEM] + [VMEM] * 6,
        out_specs=[VMEM] * 3,
        scratch_shapes=[pltpu.VMEM((4, 2, SLICE, ROWS), jnp.float32)],
        compiler_params=pltpu.CompilerParams(vmem_limit_bytes=32 * 2**20),
        cost_estimate=pl.CostEstimate(
            flops=4 * ROWS * 384 * WIDE, bytes_accessed=4000000, transcendentals=0
        ),
    )(where, grad_all.reshape(2, ROWS, WIDE + EXTRA), w_down, preact, w_up, gain_t, gs_t)


def chip_kernel(where_ref, own_ref, sums_ref, got_ref, one_ref, two_ref, three_ref, keep_ref, all_ref, hold_ref):
    yhi = where_ref[2]
    hold_ref[...] = own_ref[...] + got_ref[: 4 * SLICE].astype(jnp.float32).reshape(4, SLICE, ROWS)
    got_h, got_hs = read_sums(got_ref, 4 * SLICE)
    sum_h = sums_ref[0:1] + got_h
    sum_hs = sums_ref[1:2] + got_hs
    for step, ref in enumerate((one_ref, two_ref, three_ref), 1):
        ref[:SLICE] = hold_ref[lax.rem(yhi + step, 4)].astype(jnp.bfloat16)
        write_sums(ref, SLICE, sum_h, sum_hs)
    keep_ref[...] = hold_ref[yhi]
    all_ref[...] = jnp.concatenate([sum_h, sum_hs, jnp.zeros((6, ROWS), jnp.float32)], axis=0)


def chip_rows(where, own_blocks, own_sums, got):
    return pl.pallas_call(
        chip_kernel,
        out_shape=[jax.ShapeDtypeStruct((SLICE + 16, ROWS), jnp.bfloat16)] * 3
        + [
            jax.ShapeDtypeStruct((SLICE, ROWS), jnp.float32),
            jax.ShapeDtypeStruct((8, ROWS), jnp.float32),
        ],
        in_specs=[SMEM] + [VMEM] * 3,
        out_specs=[VMEM] * 5,
        scratch_shapes=[pltpu.VMEM((4, SLICE, ROWS), jnp.float32)],
        compiler_params=pltpu.CompilerParams(vmem_limit_bytes=16 * 2**20),
        cost_estimate=pl.CostEstimate(flops=1000000, bytes_accessed=1000000, transcendentals=0),
    )(where, own_blocks, own_sums, got)


def fore_kernel(where_ref, part_ref, got_ref, one_ref, two_ref, three_ref, keep_ref):
    core = where_ref[1]
    yhi = where_ref[2]

    def chip(at):
        return part_ref[at, core] + got_ref[at].astype(jnp.float32)

    for step, ref in enumerate((one_ref, two_ref, three_ref), 1):
        ref[...] = chip(lax.rem(yhi + step, 4)).astype(jnp.bfloat16)
    keep_ref[...] = chip(yhi)


def fore_chip(where, part, got):
    return call(
        fore_kernel,
        [((IMG, WIDE), jnp.bfloat16)] * 3 + [((IMG, WIDE), jnp.float32)],
        1,
        1000000,
        1500000,
        where,
        part,
        got,
    )


def img_kernel(keep_ref, one_ref, two_ref, three_ref, own_ref, ids_ref, send_ref, unit_ref, norm_ref):
    summed = keep_ref[...] + own_ref[...]
    for ref in (one_ref, two_ref, three_ref):
        summed = summed + ref[...].astype(jnp.float32)
    norm = jnp.sqrt(jnp.sum(summed * summed, axis=1, keepdims=True) + 1e-06)
    unit = summed / norm
    unit_ref[...] = unit
    norm_ref[...] = norm
    send_ref[:, :WIDE] = unit.astype(jnp.bfloat16)
    send_ref[:, WIDE:] = ids_ref[...]


def img_rows(keep, gots, own, ids):
    return call(
        img_kernel,
        [
            ((IMG, WIDE + EXTRA), jnp.bfloat16),
            ((IMG, WIDE), jnp.float32),
            ((IMG, 1), jnp.float32),
        ],
        0,
        200000,
        500000,
        keep,
        *gots,
        own,
        ids,
    )


def last_kernel(
    keep_ref, all_ref, one_ref, two_ref, three_ref, inv_ref, invgain_ref, invscaled_ref, grad_ref, got_ref, out_ref, down_ref, loss_ref
):
    total = keep_ref[...]
    sum_h = all_ref[0:1]
    sum_hs = all_ref[1:2]
    for ref in (one_ref, two_ref, three_ref):
        total = total + ref[:SLICE].astype(jnp.float32)
        got_h, got_hs = read_sums(ref, SLICE)
        sum_h = sum_h + got_h
        sum_hs = sum_hs + got_hs
    side = (
        invgain_ref[...] * total
        - inv_ref[:1] * (sum_h / WIDE)
        - invscaled_ref[...] * (sum_hs / WIDE)
    )
    out_ref[...] = (grad_ref[...].astype(jnp.float32) + side).astype(jnp.bfloat16)
    summed = jnp.sum(got_ref[...].astype(jnp.float32), axis=0)
    for piece in range(3):
        down_ref[:, piece * 128 : (piece + 1) * 128] = summed[piece * 24 : (piece + 1) * 24]
    tail = jnp.sum(summed[72:], axis=1, keepdims=True)
    loss_ref[...] = jnp.sum(tail, axis=0, keepdims=True) / BATCH


def last_rows(keep, sums, gots, inverse_t, invgain, invscaled, grad_own, down_got):
    return call(
        last_kernel,
        [
            ((SLICE, ROWS), jnp.bfloat16),
            ((24, 384), jnp.float32),
            ((1, 1), jnp.float32),
        ],
        0,
        1000000,
        1600000,
        keep,
        sums,
        *gots,
        inverse_t,
        invgain,
        invscaled,
        grad_own,
        down_got,
    )


def down_kernel(ylo_ref, grad_ref, hidden_ref, other_ref, out_ref):
    even = ylo_ref[0] == 0
    rows = grad_ref[:, :WIDE]
    mine = hidden_ref[...]
    other = other_ref[...]
    hidden = jnp.concatenate(
        [jnp.where(even, mine, other), jnp.where(even, other, mine)], axis=0
    )
    for piece in range(3):
        part = lax.dot_general(
            rows,
            hidden[:, piece * 128 : (piece + 1) * 128],
            (((0,), (0,)), ((), ())),
            preferred_element_type=jnp.float32,
        ).reshape(32, 2, 24, 128)
        out_ref[:, piece * 24 : (piece + 1) * 24, :] = jnp.where(
            even, part[:, 0], part[:, 1]
        ).astype(jnp.bfloat16)
    tail = grad_ref[:, WIDE:].astype(jnp.float32)
    total = jnp.sum(tail, axis=0, keepdims=True)
    first = total.astype(jnp.bfloat16).astype(jnp.float32)
    second = (total - first).astype(jnp.bfloat16).astype(jnp.float32)
    third = total - first - second
    place = lax.broadcasted_iota(jnp.int32, (8, 128), 0)
    block = jnp.where(
        place == 0, first, jnp.where(place == 1, second, jnp.where(place == 2, third, 0.0))
    )
    out_ref[:, 72:, :] = jnp.broadcast_to(block[None], (32, 8, 128)).astype(jnp.bfloat16)


def down_block(ylo, grad_all, hidden, hidden_other):
    return pl.pallas_call(
        down_kernel,
        out_shape=jax.ShapeDtypeStruct((32, 80, 128), jnp.bfloat16),
        in_specs=[
            pl.BlockSpec(memory_space=pltpu.SMEM),
            pl.BlockSpec(memory_space=pltpu.VMEM),
            pl.BlockSpec(memory_space=pltpu.VMEM),
            pl.BlockSpec(memory_space=pltpu.VMEM),
        ],
        out_specs=pl.BlockSpec(memory_space=pltpu.VMEM),
        compiler_params=pltpu.CompilerParams(vmem_limit_bytes=24 * 2**20),
        cost_estimate=pl.CostEstimate(
            flops=2 * 256 * WIDE * 384, bytes_accessed=1700000, transcendentals=0
        ),
    )(ylo.reshape(1).astype(jnp.int32), grad_all, hidden, hidden_other)


def turn(step):
    return [(at, (at + step) % 4) for at in range(4)]


def shards(
    pooled,
    ln_gain,
    ln_bias,
    w_up,
    b_up,
    w_down,
    b_down,
    text_embed,
    image_ids,
    text_ids,
    logit_scale,
    logit_bias,
    loss_scale,
):
    tens = lax.axis_index(TENS)
    row0 = tens * IMG
    col0 = tens * SLICE

    both = lax.all_gather(
        jnp.concatenate([pooled, text_embed], axis=0), TENS, axis=1, tiled=True
    )
    rows = lax.dynamic_slice_in_dim(
        both.reshape(2, ROWS, WIDE), row0, IMG, 1
    ).astype(jnp.float32)
    own, txt_rows = rows[0], rows[1]
    txt_norm = jnp.sqrt(jnp.sum(txt_rows * txt_rows, axis=1, keepdims=True) + 1e-06)
    txt_low = (txt_rows / txt_norm).astype(jnp.bfloat16)
    txt_send = jnp.concatenate([txt_low, id_columns(text_ids, row0)], axis=1)
    wide = both[:ROWS].astype(jnp.float32)
    average = jnp.mean(wide, axis=1, keepdims=True)
    centered = wide - average
    inverse = lax.rsqrt(jnp.mean(centered * centered, axis=1, keepdims=True) + 1e-06)
    scaled = centered * inverse
    normed = (scaled * ln_gain + ln_bias).astype(jnp.bfloat16)
    preact = jnp.dot(normed, w_up, preferred_element_type=jnp.float32) + b_up
    hidden = gelu_fn(preact).astype(jnp.bfloat16)
    bias_row = lax.dynamic_update_slice_in_dim(
        jnp.zeros((WIDE,), jnp.float32), b_down, col0, 0
    )
    part = jnp.dot(hidden, w_down, preferred_element_type=jnp.float32) + bias_row
    core = lax.axis_index("core")
    yhi = lax.axis_index("yhi")
    part = part.reshape(4, 2, IMG, WIDE)
    part_other = lax.dynamic_index_in_dim(part, 1 - core, 1, keepdims=False).astype(jnp.bfloat16)
    part_other, txt_send = lax.optimization_barrier((part_other, txt_send))
    core_got = lax.ppermute(
        part_other,
        "core",
        [(0, 1), (1, 0)],
    )
    txt_copies = jnp.broadcast_to(txt_send[None], (32, IMG, WIDE + EXTRA))
    txt_all = lax.all_to_all(
        txt_copies, ("x", "z"), split_axis=0, concat_axis=0, tiled=True
    ).reshape(4 * ROWS, WIDE + EXTRA)
    where = jnp.stack([lax.axis_index("ylo"), core, yhi]).astype(jnp.int32)
    sends = fore_chip(where, part, core_got)
    gots = [lax.ppermute(sends[step - 1], "yhi", turn(step)) for step in range(1, 4)]
    img_send, img_unit, img_norm = img_rows(sends[3], gots, own, id_columns(image_ids, row0))
    img_all = lax.all_gather(img_send, RING, axis=0, tiled=True)

    scalars = (logit_scale, logit_bias, loss_scale)
    other_part, other_loss = pair_rows(1 - core, scalars, img_all, txt_all)
    from_other = lax.ppermute(other_part, "core", [(0, 1), (1, 0)])
    chip_part, own_loss = pair_rows(core, scalars, img_all, txt_all, from_other)
    scaled_late, own_loss = lax.optimization_barrier((scaled, own_loss))
    gain_t = jnp.broadcast_to(ln_gain[:, None], (WIDE, ROWS))
    gs_t = gain_t * scaled_late.T
    hidden_late, gs_t = lax.optimization_barrier((hidden, gs_t))
    hidden_other = lax.ppermute(hidden_late, "ylo", [(0, 1), (1, 0)])
    ylo = lax.axis_index("ylo")
    unit_parts = lax.all_to_all(
        chip_part, ("ylo", "yhi"), split_axis=0, concat_axis=0, tiled=True
    )
    grad_unit = jnp.sum(unit_parts.reshape(8, IMG, WIDE).astype(jnp.float32), axis=0)
    tangent = jnp.sum(img_unit * grad_unit, axis=1, keepdims=True)
    grad_low = ((grad_unit - img_unit * tangent) / img_norm).astype(jnp.bfloat16)
    loss_part = jnp.sum(other_loss + own_loss, axis=0)
    loss_block = jnp.pad(pieces(loss_part, 3), ((0, IMG - 3), (0, 0)))
    grad_send = jnp.concatenate([grad_low, loss_block], axis=1)
    grad_send, hidden_other = lax.optimization_barrier((grad_send, hidden_other))
    grad_all = lax.all_gather(grad_send, RING, axis=0, tiled=True)
    send, own_blocks, own_sums = back_rows(
        where, grad_all, w_down, preact, w_up, gain_t, gs_t
    )
    grad_late, send = lax.optimization_barrier((grad_all, send))
    down_send = down_block(ylo, grad_late, hidden, hidden_other)
    down_got = lax.all_to_all(down_send, ("x", "z"), split_axis=0, concat_axis=0, tiled=True)
    got = lax.ppermute(send, "core", [(0, 1), (1, 0)])
    sends = chip_rows(where, own_blocks, own_sums, got)
    gots = [lax.ppermute(sends[step - 1], "yhi", turn(step)) for step in range(1, 4)]
    gain_own = lax.dynamic_slice_in_dim(ln_gain, col0, SLICE, 0)
    scaled_own = ((pooled.astype(jnp.float32) - average) * inverse).T
    inverse_t = jnp.broadcast_to(inverse.reshape(1, ROWS), (8, ROWS))
    grad_own = lax.dynamic_slice(grad_all, (ylo * ROWS, col0), (ROWS, SLICE))
    grad_pooled, grad_down, loss = last_rows(
        sends[3], sends[4], gots, inverse_t, inverse_t[:1] * gain_own[:, None],
        inverse_t[:1] * scaled_own, grad_own.T, down_got,
    )
    return (loss.reshape(1), grad_pooled.T, grad_down.T)


def solution(mesh):
    inner = Mesh(mesh.devices.reshape(4, 8, 2, 4, 2), DATA + TENS)
    placed = (
        P(DATA, TENS),
        P(),
        P(),
        P(None, TENS),
        P(TENS),
        P(TENS, None),
        P(TENS),
        P(DATA, TENS),
        P(DATA),
        P(DATA),
        P(),
        P(),
        P(),
    )
    return jax.shard_map(
        shards,
        mesh=inner,
        in_specs=placed,
        out_specs=(P(), P(DATA, TENS), P(TENS, DATA)),
        check_vma=False,
    )
```

```python
import jax
import jax.numpy as jnp
from jax import lax
from jax.experimental import pallas as pl
from jax.experimental.pallas import tpu as pltpu
from jax.sharding import Mesh, PartitionSpec as P

ROWS = 128
WIDE = 1536
SLICE = 192
EXTRA = 128
IMG = 16
BATCH = 8192
DATA = ("x", "z", "ylo")
TENS = ("yhi", "core")
RING = ("ylo", "yhi", "core")


def gelu_fn(values):
    return jax.nn.gelu(values, approximate=True)


def id_columns(ids, start):
    lanes = lax.broadcasted_iota(jnp.int32, (IMG, ROWS), 1)
    rows = lax.broadcasted_iota(jnp.int32, (IMG, ROWS), 0)
    own = jnp.sum(
        jnp.where(lanes == rows + start, ids[None, :], 0).astype(jnp.float32), axis=1, keepdims=True
    )
    high = jnp.floor(own / 128.0)
    low = own - 128.0 * high
    place = lax.broadcasted_iota(jnp.int32, (IMG, EXTRA), 1)
    return jnp.where(place == 0, high, jnp.where(place == 1, low, 0.0)).astype(jnp.bfloat16)


def pieces(values, count):
    parts = []
    for _ in range(count):
        part = lax.reduce_precision(values, 8, 7)
        parts.append(part.astype(jnp.bfloat16))
        values = values - part
    return jnp.stack(parts)


VMEM = pl.BlockSpec(memory_space=pltpu.VMEM)
SMEM = pl.BlockSpec(memory_space=pltpu.SMEM)


def call(kernel, outs, n_smem, flops, moved, *args):
    return pl.pallas_call(
        kernel,
        out_shape=[jax.ShapeDtypeStruct(shape, kind) for shape, kind in outs],
        in_specs=[SMEM] * n_smem + [VMEM] * (len(args) - n_smem),
        out_specs=[VMEM] * len(outs),
        compiler_params=pltpu.CompilerParams(vmem_limit_bytes=32 * 2**20),
        cost_estimate=pl.CostEstimate(flops=flops, bytes_accessed=moved, transcendentals=0),
    )(*args)


def split_two(values):
    first = values.astype(jnp.bfloat16).astype(jnp.float32)
    return first, values - first


def pair_kernel(which_ref, temper_ref, offset_ref, factor_ref, img_ref, txt_ref, *refs):
    out_ref, loss_ref = refs[-2:]
    img = img_ref[:, which_ref[0]].reshape(ROWS, WIDE + EXTRA)
    txt = txt_ref[:, :WIDE]
    across = (((1,), (1,)), ((), ()))
    scores = lax.dot_general(img[:, :WIDE], txt, across, preferred_element_type=jnp.float32)
    place = lax.broadcasted_iota(jnp.int32, (8, EXTRA), 1)
    pick = jnp.where(place == 0, 128.0, jnp.where(place == 1, 1.0, 0.0))
    txt_ids = lax.dot_general(
        pick.astype(jnp.bfloat16), txt_ref[:, WIDE:], across, preferred_element_type=jnp.float32
    )[:1]
    img_ids = jnp.sum(img[:, WIDE:].astype(jnp.float32) * pick[:1], axis=1, keepdims=True)
    temper = temper_ref[0]
    logits = temper * scores + offset_ref[0]
    positive = img_ids == txt_ids
    margin = jnp.where(positive, -logits, logits)
    shrunk = jnp.exp(-jnp.abs(margin))
    losses = jnp.maximum(margin, 0.0) + jnp.log1p(shrunk)
    sigmoid = jnp.where(margin >= 0.0, 1.0, shrunk) / (1.0 + shrunk)
    scale = temper * (factor_ref[0] / BATCH)
    weights = (jnp.where(positive, -scale, scale) * sigmoid).astype(jnp.bfloat16)
    part = jnp.dot(weights, txt, preferred_element_type=jnp.float32)
    if len(refs) == 3:
        part = part + refs[0][...].astype(jnp.float32)
    out_ref[...] = part.astype(jnp.bfloat16)
    folded = losses[:, :128] + losses[:, 128:256] + losses[:, 256:384] + losses[:, 384:]
    loss_ref[...] = jnp.sum(folded.reshape(16, 8, 128), axis=0)


def pair_rows(which, scalars, img_all, txt_all, *added):
    return call(
        pair_kernel,
        [((ROWS, WIDE), jnp.bfloat16), ((8, 128), jnp.float32)],
        4,
        4 * ROWS * 512 * WIDE,
        3000000,
        which.reshape(1).astype(jnp.int32),
        *scalars,
        img_all.reshape(8, 2, IMG, WIDE + EXTRA),
        txt_all,
        *added,
    )


def gelu_slope(values):
    root = 0.7978845608028654
    inner = jnp.tanh(root * (values + 0.044715 * (values * values * values)))
    return 0.5 * (1.0 + inner) + 0.5 * values * (1.0 - inner * inner) * root * (
        1.0 + 3.0 * 0.044715 * (values * values)
    )


def back_kernel(
    where_ref, grad_ref, down_ref, pre_ref, up_ref, gain_ref, gs_ref, send_ref, own_ref, sum_ref, hold_ref
):
    across = (((1,), (1,)), ((), ()))
    core = where_ref[1]
    first = where_ref[0] * 4
    grad = jnp.concatenate(
        [grad_ref[side, first + at, :, :WIDE] for at in range(4) for side in range(2)], axis=0
    )
    grad_hidden = lax.dot_general(grad, down_ref[...], across, preferred_element_type=jnp.float32)
    grad_pre = (grad_hidden * gelu_slope(pre_ref[...])).astype(jnp.bfloat16)
    part = lax.dot_general(up_ref[...], grad_pre, across, preferred_element_type=jnp.float32)
    hold_ref[...] = part.reshape(4, 2, SLICE, ROWS)
    sum_h = jnp.sum(part * gain_ref[...], axis=0, keepdims=True)
    sum_hs = jnp.sum(part * gs_ref[...], axis=0, keepdims=True)
    send_ref[: 4 * SLICE] = hold_ref[:, 1 - core].reshape(4 * SLICE, ROWS).astype(jnp.bfloat16)
    own_ref[...] = hold_ref[:, core]
    write_sums(send_ref, 4 * SLICE, sum_h, sum_hs)
    sum_ref[...] = jnp.concatenate([sum_h, sum_hs, jnp.zeros((6, ROWS), jnp.float32)], axis=0)


def write_sums(ref, start, sum_h, sum_hs):
    h_hi, h_lo = split_two(sum_h)
    s_hi, s_lo = split_two(sum_hs)
    ref[start:] = jnp.concatenate(
        [h_hi, s_hi, h_lo, s_lo, jnp.zeros((12, ROWS), jnp.float32)], axis=0
    ).astype(jnp.bfloat16)


def read_sums(ref, start):
    block = ref[start:].astype(jnp.float32)
    return block[0:1] + block[2:3], block[1:2] + block[3:4]


def back_rows(where, grad_all, w_down, preact, w_up, gain_t, gs_t):
    return pl.pallas_call(
        back_kernel,
        out_shape=[
            jax.ShapeDtypeStruct((4 * SLICE + 16, ROWS), jnp.bfloat16),
            jax.ShapeDtypeStruct((4, SLICE, ROWS), jnp.float32),
            jax.ShapeDtypeStruct((8, ROWS), jnp.float32),
        ],
        in_specs=[SMEM] + [VMEM] * 6,
        out_specs=[VMEM] * 3,
        scratch_shapes=[pltpu.VMEM((4, 2, SLICE, ROWS), jnp.float32)],
        compiler_params=pltpu.CompilerParams(vmem_limit_bytes=32 * 2**20),
        cost_estimate=pl.CostEstimate(
            flops=4 * ROWS * 384 * WIDE, bytes_accessed=4000000, transcendentals=0
        ),
    )(where, grad_all, w_down, preact, w_up, gain_t, gs_t)


def chip_kernel(where_ref, own_ref, sums_ref, got_ref, one_ref, two_ref, three_ref, keep_ref, all_ref, hold_ref):
    yhi = where_ref[2]
    hold_ref[...] = own_ref[...] + got_ref[: 4 * SLICE].astype(jnp.float32).reshape(4, SLICE, ROWS)
    got_h, got_hs = read_sums(got_ref, 4 * SLICE)
    sum_h = sums_ref[0:1] + got_h
    sum_hs = sums_ref[1:2] + got_hs
    for step, ref in enumerate((one_ref, two_ref, three_ref), 1):
        ref[:SLICE] = hold_ref[lax.rem(yhi + step, 4)].astype(jnp.bfloat16)
        write_sums(ref, SLICE, sum_h, sum_hs)
    keep_ref[...] = hold_ref[yhi]
    all_ref[...] = jnp.concatenate([sum_h, sum_hs, jnp.zeros((6, ROWS), jnp.float32)], axis=0)


def chip_rows(where, own_blocks, own_sums, got):
    return pl.pallas_call(
        chip_kernel,
        out_shape=[jax.ShapeDtypeStruct((SLICE + 16, ROWS), jnp.bfloat16)] * 3
        + [
            jax.ShapeDtypeStruct((SLICE, ROWS), jnp.float32),
            jax.ShapeDtypeStruct((8, ROWS), jnp.float32),
        ],
        in_specs=[SMEM] + [VMEM] * 3,
        out_specs=[VMEM] * 5,
        scratch_shapes=[pltpu.VMEM((4, SLICE, ROWS), jnp.float32)],
        compiler_params=pltpu.CompilerParams(vmem_limit_bytes=16 * 2**20),
        cost_estimate=pl.CostEstimate(flops=1000000, bytes_accessed=1000000, transcendentals=0),
    )(where, own_blocks, own_sums, got)


def fore_kernel(where_ref, part_ref, got_ref, one_ref, two_ref, three_ref, keep_ref):
    core = where_ref[1]
    yhi = where_ref[2]

    def chip(at):
        return part_ref[at, core] + got_ref[at].astype(jnp.float32)

    for step, ref in enumerate((one_ref, two_ref, three_ref), 1):
        ref[...] = chip(lax.rem(yhi + step, 4)).astype(jnp.bfloat16)
    keep_ref[...] = chip(yhi)


def fore_chip(where, part, got):
    return call(
        fore_kernel,
        [((IMG, WIDE), jnp.bfloat16)] * 3 + [((IMG, WIDE), jnp.float32)],
        1,
        1000000,
        1500000,
        where,
        part,
        got,
    )


def img_kernel(keep_ref, one_ref, two_ref, three_ref, own_ref, ids_ref, send_ref, unit_ref, norm_ref):
    summed = keep_ref[...] + own_ref[...]
    for ref in (one_ref, two_ref, three_ref):
        summed = summed + ref[...].astype(jnp.float32)
    norm = jnp.sqrt(jnp.sum(summed * summed, axis=1, keepdims=True) + 1e-06)
    unit = summed / norm
    unit_ref[...] = unit
    norm_ref[...] = norm
    send_ref[:, :WIDE] = unit.astype(jnp.bfloat16)
    send_ref[:, WIDE:] = ids_ref[...]


def img_rows(keep, gots, own, ids):
    return call(
        img_kernel,
        [
            ((IMG, WIDE + EXTRA), jnp.bfloat16),
            ((IMG, WIDE), jnp.float32),
            ((IMG, 1), jnp.float32),
        ],
        0,
        200000,
        500000,
        keep,
        *gots,
        own,
        ids,
    )


def last_kernel(
    keep_ref, all_ref, one_ref, two_ref, three_ref, inv_ref, invgain_ref, invscaled_ref, grad_ref, got_ref, out_ref, down_ref, loss_ref
):
    total = keep_ref[...]
    sum_h = all_ref[0:1]
    sum_hs = all_ref[1:2]
    for ref in (one_ref, two_ref, three_ref):
        total = total + ref[:SLICE].astype(jnp.float32)
        got_h, got_hs = read_sums(ref, SLICE)
        sum_h = sum_h + got_h
        sum_hs = sum_hs + got_hs
    side = (
        invgain_ref[...] * total
        - inv_ref[:1] * (sum_h / WIDE)
        - invscaled_ref[...] * (sum_hs / WIDE)
    )
    out_ref[...] = (grad_ref[...].astype(jnp.float32) + side).astype(jnp.bfloat16)
    summed = jnp.sum(got_ref[...].astype(jnp.float32), axis=0)
    for piece in range(3):
        down_ref[:, piece * 128 : (piece + 1) * 128] = summed[piece * 24 : (piece + 1) * 24]
    tail = jnp.sum(summed[72:], axis=1, keepdims=True)
    loss_ref[...] = jnp.sum(tail, axis=0, keepdims=True) / BATCH


def last_rows(keep, sums, gots, inverse_t, invgain, invscaled, grad_own, down_got):
    return call(
        last_kernel,
        [
            ((SLICE, ROWS), jnp.bfloat16),
            ((24, 384), jnp.float32),
            ((1, 1), jnp.float32),
        ],
        0,
        1000000,
        1600000,
        keep,
        sums,
        *gots,
        inverse_t,
        invgain,
        invscaled,
        grad_own,
        down_got,
    )


def down_kernel(ylo_ref, grad_ref, hidden_ref, other_ref, out_ref):
    even = ylo_ref[0] == 0
    rows = jnp.concatenate(
        [grad_ref[side, at, :, :WIDE] for at in range(8) for side in range(2)], axis=0
    )
    mine = hidden_ref[...]
    other = other_ref[...]
    hidden = jnp.concatenate(
        [jnp.where(even, mine, other), jnp.where(even, other, mine)], axis=0
    )
    for piece in range(3):
        part = lax.dot_general(
            rows,
            hidden[:, piece * 128 : (piece + 1) * 128],
            (((0,), (0,)), ((), ())),
            preferred_element_type=jnp.float32,
        ).reshape(32, 2, 24, 128)
        out_ref[:, piece * 24 : (piece + 1) * 24, :] = jnp.where(
            even, part[:, 0], part[:, 1]
        ).astype(jnp.bfloat16)
    tail = grad_ref[:, :, :, WIDE:].astype(jnp.float32).reshape(256, EXTRA)
    total = jnp.sum(tail, axis=0, keepdims=True)
    first = total.astype(jnp.bfloat16).astype(jnp.float32)
    second = (total - first).astype(jnp.bfloat16).astype(jnp.float32)
    third = total - first - second
    place = lax.broadcasted_iota(jnp.int32, (8, 128), 0)
    block = jnp.where(
        place == 0, first, jnp.where(place == 1, second, jnp.where(place == 2, third, 0.0))
    )
    out_ref[:, 72:, :] = jnp.broadcast_to(block[None], (32, 8, 128)).astype(jnp.bfloat16)


def down_block(ylo, grad_all, hidden, hidden_other):
    return pl.pallas_call(
        down_kernel,
        out_shape=jax.ShapeDtypeStruct((32, 80, 128), jnp.bfloat16),
        in_specs=[
            pl.BlockSpec(memory_space=pltpu.SMEM),
            pl.BlockSpec(memory_space=pltpu.VMEM),
            pl.BlockSpec(memory_space=pltpu.VMEM),
            pl.BlockSpec(memory_space=pltpu.VMEM),
        ],
        out_specs=pl.BlockSpec(memory_space=pltpu.VMEM),
        compiler_params=pltpu.CompilerParams(vmem_limit_bytes=24 * 2**20),
        cost_estimate=pl.CostEstimate(
            flops=2 * 256 * WIDE * 384, bytes_accessed=1700000, transcendentals=0
        ),
    )(ylo.reshape(1).astype(jnp.int32), grad_all, hidden, hidden_other)


def turn(step):
    return [(at, (at + step) % 4) for at in range(4)]


def shards(
    pooled,
    ln_gain,
    ln_bias,
    w_up,
    b_up,
    w_down,
    b_down,
    text_embed,
    image_ids,
    text_ids,
    logit_scale,
    logit_bias,
    loss_scale,
):
    tens = lax.axis_index(TENS)
    row0 = tens * IMG
    col0 = tens * SLICE

    both = lax.all_gather(
        jnp.concatenate([pooled, text_embed], axis=0), TENS, axis=1, tiled=True
    )
    rows = lax.dynamic_slice_in_dim(
        both.reshape(2, ROWS, WIDE), row0, IMG, 1
    ).astype(jnp.float32)
    own, txt_rows = rows[0], rows[1]
    txt_norm = jnp.sqrt(jnp.sum(txt_rows * txt_rows, axis=1, keepdims=True) + 1e-06)
    txt_low = (txt_rows / txt_norm).astype(jnp.bfloat16)
    txt_send = jnp.concatenate([txt_low, id_columns(text_ids, row0)], axis=1)
    wide = both[:ROWS].astype(jnp.float32)
    average = jnp.mean(wide, axis=1, keepdims=True)
    centered = wide - average
    inverse = lax.rsqrt(jnp.mean(centered * centered, axis=1, keepdims=True) + 1e-06)
    scaled = centered * inverse
    normed = (scaled * ln_gain + ln_bias).astype(jnp.bfloat16)
    preact = jnp.dot(normed, w_up, preferred_element_type=jnp.float32) + b_up
    hidden = gelu_fn(preact).astype(jnp.bfloat16)
    bias_row = lax.dynamic_update_slice_in_dim(
        jnp.zeros((WIDE,), jnp.float32), b_down, col0, 0
    )
    part = jnp.dot(hidden, w_down, preferred_element_type=jnp.float32) + bias_row
    core = lax.axis_index("core")
    yhi = lax.axis_index("yhi")
    part = part.reshape(4, 2, IMG, WIDE)
    part_other = lax.dynamic_index_in_dim(part, 1 - core, 1, keepdims=False).astype(jnp.bfloat16)
    part_other, txt_send = lax.optimization_barrier((part_other, txt_send))
    core_got = lax.ppermute(
        part_other,
        "core",
        [(0, 1), (1, 0)],
    )
    txt_copies = jnp.broadcast_to(txt_send[None], (32, IMG, WIDE + EXTRA))
    txt_all = lax.all_to_all(
        txt_copies, ("x", "z"), split_axis=0, concat_axis=0, tiled=True
    ).reshape(4 * ROWS, WIDE + EXTRA)
    where = jnp.stack([lax.axis_index("ylo"), core, yhi]).astype(jnp.int32)
    sends = fore_chip(where, part, core_got)
    gots = [lax.ppermute(sends[step - 1], "yhi", turn(step)) for step in range(1, 4)]
    img_send, img_unit, img_norm = img_rows(sends[3], gots, own, id_columns(image_ids, row0))
    img_all = lax.all_gather(img_send, RING, axis=0, tiled=True)

    scalars = (logit_scale, logit_bias, loss_scale)
    other_part, other_loss = pair_rows(1 - core, scalars, img_all, txt_all)
    from_other = lax.ppermute(other_part, "core", [(0, 1), (1, 0)])
    chip_part, own_loss = pair_rows(core, scalars, img_all, txt_all, from_other)
    scaled_late, own_loss = lax.optimization_barrier((scaled, own_loss))
    gain_t = jnp.broadcast_to(ln_gain[:, None], (WIDE, ROWS))
    gs_t = gain_t * scaled_late.T
    hidden_late, gs_t = lax.optimization_barrier((hidden, gs_t))
    hidden_other = lax.ppermute(hidden_late, "ylo", [(0, 1), (1, 0)])
    ylo = lax.axis_index("ylo")
    unit_parts = lax.all_to_all(
        chip_part, ("ylo", "yhi"), split_axis=0, concat_axis=0, tiled=True
    )
    grad_unit = jnp.sum(unit_parts.reshape(8, IMG, WIDE).astype(jnp.float32), axis=0)
    tangent = jnp.sum(img_unit * grad_unit, axis=1, keepdims=True)
    grad_low = ((grad_unit - img_unit * tangent) / img_norm).astype(jnp.bfloat16)
    loss_part = jnp.sum(other_loss + own_loss, axis=0)
    loss_block = jnp.pad(pieces(loss_part, 3), ((0, IMG - 3), (0, 0)))
    grad_send = jnp.concatenate([grad_low, loss_block], axis=1)
    grad_send, hidden_other = lax.optimization_barrier((grad_send, hidden_other))
    grad_chips = lax.all_to_all(
        jnp.broadcast_to(grad_send[None], (8, IMG, WIDE + EXTRA)).reshape(ROWS, WIDE + EXTRA),
        ("ylo", "yhi"),
        split_axis=0,
        concat_axis=0,
        tiled=True,
    )
    grad_all = lax.all_gather(grad_chips, "core", axis=0, tiled=True).reshape(
        2, 8, IMG, WIDE + EXTRA
    )
    send, own_blocks, own_sums = back_rows(
        where, grad_all, w_down, preact, w_up, gain_t, gs_t
    )
    grad_late, send = lax.optimization_barrier((grad_all, send))
    down_send = down_block(ylo, grad_late, hidden, hidden_other)
    down_got = lax.all_to_all(down_send, ("x", "z"), split_axis=0, concat_axis=0, tiled=True)
    got = lax.ppermute(send, "core", [(0, 1), (1, 0)])
    sends = chip_rows(where, own_blocks, own_sums, got)
    gots = [lax.ppermute(sends[step - 1], "yhi", turn(step)) for step in range(1, 4)]
    gain_own = lax.dynamic_slice_in_dim(ln_gain, col0, SLICE, 0)
    scaled_own = ((pooled.astype(jnp.float32) - average) * inverse).T
    inverse_t = jnp.broadcast_to(inverse.reshape(1, ROWS), (8, ROWS))
    grad_own = (
        lax.dynamic_slice(grad_all, (0, ylo * 4, 0, col0), (2, 4, IMG, SLICE))
        .transpose(1, 0, 2, 3)
        .reshape(ROWS, SLICE)
    )
    grad_pooled, grad_down, loss = last_rows(
        sends[3], sends[4], gots, inverse_t, inverse_t[:1] * gain_own[:, None],
        inverse_t[:1] * scaled_own, grad_own.T, down_got,
    )
    return (loss.reshape(1), grad_pooled.T, grad_down.T)


def solution(mesh):
    inner = Mesh(mesh.devices.reshape(4, 8, 2, 4, 2), DATA + TENS)
    placed = (
        P(DATA, TENS),
        P(),
        P(),
        P(None, TENS),
        P(TENS),
        P(TENS, None),
        P(TENS),
        P(DATA, TENS),
        P(DATA),
        P(DATA),
        P(),
        P(),
        P(),
    )
    return jax.shard_map(
        shards,
        mesh=inner,
        in_specs=placed,
        out_specs=(P(), P(DATA, TENS), P(TENS, DATA)),
        check_vma=False,
    )
```

```python
import jax
import jax.numpy as jnp
from jax import lax
from jax.experimental import pallas as pl
from jax.experimental.pallas import tpu as pltpu
from jax.sharding import Mesh, PartitionSpec as P

ROWS = 128
WIDE = 1536
SLICE = 192
EXTRA = 128
IMG = 16
BATCH = 8192
DATA = ("x", "z", "ylo")
TENS = ("yhi", "core")
RING = ("ylo", "yhi", "core")


def gelu_fn(values):
    return jax.nn.gelu(values, approximate=True)


def id_columns(ids, start):
    lanes = lax.broadcasted_iota(jnp.int32, (IMG, ROWS), 1)
    rows = lax.broadcasted_iota(jnp.int32, (IMG, ROWS), 0)
    own = jnp.sum(
        jnp.where(lanes == rows + start, ids[None, :], 0).astype(jnp.float32), axis=1, keepdims=True
    )
    high = jnp.floor(own / 128.0)
    low = own - 128.0 * high
    place = lax.broadcasted_iota(jnp.int32, (IMG, EXTRA), 1)
    return jnp.where(place == 0, high, jnp.where(place == 1, low, 0.0)).astype(jnp.bfloat16)


def pieces(values, count):
    parts = []
    for _ in range(count):
        part = lax.reduce_precision(values, 8, 7)
        parts.append(part.astype(jnp.bfloat16))
        values = values - part
    return jnp.stack(parts)


VMEM = pl.BlockSpec(memory_space=pltpu.VMEM)
SMEM = pl.BlockSpec(memory_space=pltpu.SMEM)


def call(kernel, outs, n_smem, flops, moved, *args):
    return pl.pallas_call(
        kernel,
        out_shape=[jax.ShapeDtypeStruct(shape, kind) for shape, kind in outs],
        in_specs=[SMEM] * n_smem + [VMEM] * (len(args) - n_smem),
        out_specs=[VMEM] * len(outs),
        compiler_params=pltpu.CompilerParams(vmem_limit_bytes=32 * 2**20),
        cost_estimate=pl.CostEstimate(flops=flops, bytes_accessed=moved, transcendentals=0),
    )(*args)


def split_two(values):
    first = values.astype(jnp.bfloat16).astype(jnp.float32)
    return first, values - first


def pair_kernel(which_ref, temper_ref, offset_ref, factor_ref, img_ref, txt_ref, *refs):
    out_ref, loss_ref = refs[-2:]
    img = img_ref[:, which_ref[0]].reshape(ROWS, WIDE + EXTRA)
    txt = txt_ref[:, :WIDE]
    across = (((1,), (1,)), ((), ()))
    scores = lax.dot_general(img[:, :WIDE], txt, across, preferred_element_type=jnp.float32)
    place = lax.broadcasted_iota(jnp.int32, (8, EXTRA), 1)
    pick = jnp.where(place == 0, 128.0, jnp.where(place == 1, 1.0, 0.0))
    txt_ids = lax.dot_general(
        pick.astype(jnp.bfloat16), txt_ref[:, WIDE:], across, preferred_element_type=jnp.float32
    )[:1]
    img_ids = jnp.sum(img[:, WIDE:].astype(jnp.float32) * pick[:1], axis=1, keepdims=True)
    temper = temper_ref[0]
    logits = temper * scores + offset_ref[0]
    positive = img_ids == txt_ids
    margin = jnp.where(positive, -logits, logits)
    shrunk = jnp.exp(-jnp.abs(margin))
    losses = jnp.maximum(margin, 0.0) + jnp.log1p(shrunk)
    sigmoid = jnp.where(margin >= 0.0, 1.0, shrunk) / (1.0 + shrunk)
    scale = temper * (factor_ref[0] / BATCH)
    weights = (jnp.where(positive, -scale, scale) * sigmoid).astype(jnp.bfloat16)
    part = jnp.dot(weights, txt, preferred_element_type=jnp.float32)
    if len(refs) == 3:
        part = part + refs[0][...].astype(jnp.float32)
    out_ref[...] = part.astype(jnp.bfloat16)
    folded = losses[:, :128] + losses[:, 128:256] + losses[:, 256:384] + losses[:, 384:]
    loss_ref[...] = jnp.sum(folded.reshape(16, 8, 128), axis=0)


def pair_rows(which, scalars, img_all, txt_all, *added):
    return call(
        pair_kernel,
        [((ROWS, WIDE), jnp.bfloat16), ((8, 128), jnp.float32)],
        4,
        4 * ROWS * 512 * WIDE,
        3000000,
        which.reshape(1).astype(jnp.int32),
        *scalars,
        img_all.reshape(8, 2, IMG, WIDE + EXTRA),
        txt_all,
        *added,
    )


def gelu_slope(values):
    root = 0.7978845608028654
    inner = jnp.tanh(root * (values + 0.044715 * (values * values * values)))
    return 0.5 * (1.0 + inner) + 0.5 * values * (1.0 - inner * inner) * root * (
        1.0 + 3.0 * 0.044715 * (values * values)
    )


def back_kernel(
    where_ref, grad_ref, down_ref, pre_ref, up_ref, gain_ref, gs_ref, send_ref, own_ref, sum_ref, hold_ref
):
    across = (((1,), (1,)), ((), ()))
    core = where_ref[1]
    first = where_ref[0] * 4
    grad = jnp.concatenate(
        [grad_ref[side, first + at, :, :WIDE] for at in range(4) for side in range(2)], axis=0
    )
    grad_hidden = lax.dot_general(grad, down_ref[...], across, preferred_element_type=jnp.float32)
    grad_pre = (grad_hidden * gelu_slope(pre_ref[...])).astype(jnp.bfloat16)
    part = lax.dot_general(up_ref[...], grad_pre, across, preferred_element_type=jnp.float32)
    hold_ref[...] = part.reshape(4, 2, SLICE, ROWS)
    sum_h = jnp.sum(part * gain_ref[...], axis=0, keepdims=True)
    sum_hs = jnp.sum(part * gs_ref[...], axis=0, keepdims=True)
    send_ref[: 4 * SLICE] = hold_ref[:, 1 - core].reshape(4 * SLICE, ROWS).astype(jnp.bfloat16)
    own_ref[...] = hold_ref[:, core]
    write_sums(send_ref, 4 * SLICE, sum_h, sum_hs)
    sum_ref[...] = jnp.concatenate([sum_h, sum_hs, jnp.zeros((6, ROWS), jnp.float32)], axis=0)


def write_sums(ref, start, sum_h, sum_hs):
    h_hi, h_lo = split_two(sum_h)
    s_hi, s_lo = split_two(sum_hs)
    ref[start:] = jnp.concatenate(
        [h_hi, s_hi, h_lo, s_lo, jnp.zeros((12, ROWS), jnp.float32)], axis=0
    ).astype(jnp.bfloat16)


def read_sums(ref, start):
    block = ref[start:].astype(jnp.float32)
    return block[0:1] + block[2:3], block[1:2] + block[3:4]


def back_rows(where, grad_all, w_down, preact, w_up, gain_t, gs_t):
    return pl.pallas_call(
        back_kernel,
        out_shape=[
            jax.ShapeDtypeStruct((4 * SLICE + 16, ROWS), jnp.bfloat16),
            jax.ShapeDtypeStruct((4, SLICE, ROWS), jnp.float32),
            jax.ShapeDtypeStruct((8, ROWS), jnp.float32),
        ],
        in_specs=[SMEM] + [VMEM] * 6,
        out_specs=[VMEM] * 3,
        scratch_shapes=[pltpu.VMEM((4, 2, SLICE, ROWS), jnp.float32)],
        compiler_params=pltpu.CompilerParams(vmem_limit_bytes=32 * 2**20),
        cost_estimate=pl.CostEstimate(
            flops=4 * ROWS * 384 * WIDE, bytes_accessed=4000000, transcendentals=0
        ),
    )(where, grad_all, w_down, preact, w_up, gain_t, gs_t)


def chip_kernel(where_ref, own_ref, sums_ref, got_ref, one_ref, two_ref, three_ref, keep_ref, all_ref, hold_ref):
    yhi = where_ref[2]
    hold_ref[...] = own_ref[...] + got_ref[: 4 * SLICE].astype(jnp.float32).reshape(4, SLICE, ROWS)
    got_h, got_hs = read_sums(got_ref, 4 * SLICE)
    sum_h = sums_ref[0:1] + got_h
    sum_hs = sums_ref[1:2] + got_hs
    for step, ref in enumerate((one_ref, two_ref, three_ref), 1):
        ref[:SLICE] = hold_ref[lax.rem(yhi + step, 4)].astype(jnp.bfloat16)
        write_sums(ref, SLICE, sum_h, sum_hs)
    keep_ref[...] = hold_ref[yhi]
    all_ref[...] = jnp.concatenate([sum_h, sum_hs, jnp.zeros((6, ROWS), jnp.float32)], axis=0)


def chip_rows(where, own_blocks, own_sums, got):
    return pl.pallas_call(
        chip_kernel,
        out_shape=[jax.ShapeDtypeStruct((SLICE + 16, ROWS), jnp.bfloat16)] * 3
        + [
            jax.ShapeDtypeStruct((SLICE, ROWS), jnp.float32),
            jax.ShapeDtypeStruct((8, ROWS), jnp.float32),
        ],
        in_specs=[SMEM] + [VMEM] * 3,
        out_specs=[VMEM] * 5,
        scratch_shapes=[pltpu.VMEM((4, SLICE, ROWS), jnp.float32)],
        compiler_params=pltpu.CompilerParams(vmem_limit_bytes=16 * 2**20),
        cost_estimate=pl.CostEstimate(flops=1000000, bytes_accessed=1000000, transcendentals=0),
    )(where, own_blocks, own_sums, got)


def fore_kernel(where_ref, part_ref, got_ref, one_ref, two_ref, three_ref, keep_ref):
    core = where_ref[1]
    yhi = where_ref[2]

    def chip(at):
        return part_ref[at, core] + got_ref[at].astype(jnp.float32)

    for step, ref in enumerate((one_ref, two_ref, three_ref), 1):
        ref[...] = chip(lax.rem(yhi + step, 4)).astype(jnp.bfloat16)
    keep_ref[...] = chip(yhi)


def fore_chip(where, part, got):
    return call(
        fore_kernel,
        [((IMG, WIDE), jnp.bfloat16)] * 3 + [((IMG, WIDE), jnp.float32)],
        1,
        1000000,
        1500000,
        where,
        part,
        got,
    )


def img_kernel(keep_ref, one_ref, two_ref, three_ref, own_ref, ids_ref, send_ref, unit_ref, norm_ref):
    summed = keep_ref[...] + own_ref[...]
    for ref in (one_ref, two_ref, three_ref):
        summed = summed + ref[...].astype(jnp.float32)
    norm = jnp.sqrt(jnp.sum(summed * summed, axis=1, keepdims=True) + 1e-06)
    unit = summed / norm
    unit_ref[...] = unit
    norm_ref[...] = norm
    send_ref[:, :WIDE] = unit.astype(jnp.bfloat16)
    send_ref[:, WIDE:] = ids_ref[...]


def img_rows(keep, gots, own, ids):
    return call(
        img_kernel,
        [
            ((IMG, WIDE + EXTRA), jnp.bfloat16),
            ((IMG, WIDE), jnp.float32),
            ((IMG, 1), jnp.float32),
        ],
        0,
        200000,
        500000,
        keep,
        *gots,
        own,
        ids,
    )


def last_kernel(
    keep_ref, all_ref, one_ref, two_ref, three_ref, inv_ref, invgain_ref, invscaled_ref, grad_ref, got_ref, out_ref, down_ref, loss_ref
):
    total = keep_ref[...]
    sum_h = all_ref[0:1]
    sum_hs = all_ref[1:2]
    for ref in (one_ref, two_ref, three_ref):
        total = total + ref[:SLICE].astype(jnp.float32)
        got_h, got_hs = read_sums(ref, SLICE)
        sum_h = sum_h + got_h
        sum_hs = sum_hs + got_hs
    side = (
        invgain_ref[...] * total
        - inv_ref[:1] * (sum_h / WIDE)
        - invscaled_ref[...] * (sum_hs / WIDE)
    )
    out_ref[...] = (grad_ref[...].astype(jnp.float32) + side).astype(jnp.bfloat16)
    summed = jnp.sum(got_ref[...].astype(jnp.float32), axis=0)
    for piece in range(3):
        down_ref[:, piece * 128 : (piece + 1) * 128] = summed[piece * 24 : (piece + 1) * 24]
    tail = jnp.sum(summed[72:], axis=1, keepdims=True)
    loss_ref[...] = jnp.sum(tail, axis=0, keepdims=True) / BATCH


def last_rows(keep, sums, gots, inverse_t, invgain, invscaled, grad_own, down_got):
    return call(
        last_kernel,
        [
            ((SLICE, ROWS), jnp.bfloat16),
            ((24, 384), jnp.float32),
            ((1, 1), jnp.float32),
        ],
        0,
        1000000,
        1600000,
        keep,
        sums,
        *gots,
        inverse_t,
        invgain,
        invscaled,
        grad_own,
        down_got,
    )


def down_kernel(ylo_ref, grad_ref, hidden_ref, other_ref, out_ref):
    even = ylo_ref[0] == 0
    rows = jnp.concatenate(
        [grad_ref[side, at, :, :WIDE] for at in range(8) for side in range(2)], axis=0
    )
    mine = hidden_ref[...]
    other = other_ref[...]
    hidden = jnp.concatenate(
        [jnp.where(even, mine, other), jnp.where(even, other, mine)], axis=0
    )
    for piece in range(3):
        part = lax.dot_general(
            rows,
            hidden[:, piece * 128 : (piece + 1) * 128],
            (((0,), (0,)), ((), ())),
            preferred_element_type=jnp.float32,
        ).reshape(32, 2, 24, 128)
        out_ref[:, piece * 24 : (piece + 1) * 24, :] = jnp.where(
            even, part[:, 0], part[:, 1]
        ).astype(jnp.bfloat16)
    tail = grad_ref[:, :, :, WIDE:].astype(jnp.float32).reshape(256, EXTRA)
    total = jnp.sum(tail, axis=0, keepdims=True)
    first = total.astype(jnp.bfloat16).astype(jnp.float32)
    second = (total - first).astype(jnp.bfloat16).astype(jnp.float32)
    third = total - first - second
    place = lax.broadcasted_iota(jnp.int32, (8, 128), 0)
    block = jnp.where(
        place == 0, first, jnp.where(place == 1, second, jnp.where(place == 2, third, 0.0))
    )
    out_ref[:, 72:, :] = jnp.broadcast_to(block[None], (32, 8, 128)).astype(jnp.bfloat16)


def down_block(ylo, grad_all, hidden, hidden_other):
    return pl.pallas_call(
        down_kernel,
        out_shape=jax.ShapeDtypeStruct((32, 80, 128), jnp.bfloat16),
        in_specs=[
            pl.BlockSpec(memory_space=pltpu.SMEM),
            pl.BlockSpec(memory_space=pltpu.VMEM),
            pl.BlockSpec(memory_space=pltpu.VMEM),
            pl.BlockSpec(memory_space=pltpu.VMEM),
        ],
        out_specs=pl.BlockSpec(memory_space=pltpu.VMEM),
        compiler_params=pltpu.CompilerParams(vmem_limit_bytes=24 * 2**20),
        cost_estimate=pl.CostEstimate(
            flops=2 * 256 * WIDE * 384, bytes_accessed=1700000, transcendentals=0
        ),
    )(ylo.reshape(1).astype(jnp.int32), grad_all, hidden, hidden_other)


def turn(step):
    return [(at, (at + step) % 4) for at in range(4)]


def shards(
    pooled,
    ln_gain,
    ln_bias,
    w_up,
    b_up,
    w_down,
    b_down,
    text_embed,
    image_ids,
    text_ids,
    logit_scale,
    logit_bias,
    loss_scale,
):
    tens = lax.axis_index(TENS)
    row0 = tens * IMG
    col0 = tens * SLICE

    both = lax.all_gather(
        jnp.concatenate([pooled, text_embed], axis=0), TENS, axis=1, tiled=True
    )
    rows = lax.dynamic_slice_in_dim(
        both.reshape(2, ROWS, WIDE), row0, IMG, 1
    ).astype(jnp.float32)
    own, txt_rows = rows[0], rows[1]
    txt_norm = jnp.sqrt(jnp.sum(txt_rows * txt_rows, axis=1, keepdims=True) + 1e-06)
    txt_low = (txt_rows / txt_norm).astype(jnp.bfloat16)
    txt_send = jnp.concatenate([txt_low, id_columns(text_ids, row0)], axis=1)
    wide = both[:ROWS].astype(jnp.float32)
    average = jnp.mean(wide, axis=1, keepdims=True)
    centered = wide - average
    inverse = lax.rsqrt(jnp.mean(centered * centered, axis=1, keepdims=True) + 1e-06)
    scaled = centered * inverse
    normed = (scaled * ln_gain + ln_bias).astype(jnp.bfloat16)
    preact = jnp.dot(normed, w_up, preferred_element_type=jnp.float32) + b_up
    hidden = gelu_fn(preact).astype(jnp.bfloat16)
    bias_row = lax.dynamic_update_slice_in_dim(
        jnp.zeros((WIDE,), jnp.float32), b_down, col0, 0
    )
    part = jnp.dot(hidden, w_down, preferred_element_type=jnp.float32) + bias_row
    core = lax.axis_index("core")
    yhi = lax.axis_index("yhi")
    part = part.reshape(4, 2, IMG, WIDE)
    part_other = lax.dynamic_index_in_dim(part, 1 - core, 1, keepdims=False).astype(jnp.bfloat16)
    part_other, txt_send = lax.optimization_barrier((part_other, txt_send))
    core_got = lax.ppermute(
        part_other,
        "core",
        [(0, 1), (1, 0)],
    )
    txt_copies = jnp.broadcast_to(txt_send[None], (32, IMG, WIDE + EXTRA))
    txt_all = lax.all_to_all(
        txt_copies, ("x", "z"), split_axis=0, concat_axis=0, tiled=True
    ).reshape(4 * ROWS, WIDE + EXTRA)
    where = jnp.stack([lax.axis_index("ylo"), core, yhi]).astype(jnp.int32)
    sends = fore_chip(where, part, core_got)
    gots = [lax.ppermute(sends[step - 1], "yhi", turn(step)) for step in (2, 1, 3)]
    img_send, img_unit, img_norm = img_rows(sends[3], gots, own, id_columns(image_ids, row0))
    img_all = lax.all_gather(img_send, RING, axis=0, tiled=True)

    scalars = (logit_scale, logit_bias, loss_scale)
    other_part, other_loss = pair_rows(1 - core, scalars, img_all, txt_all)
    from_other = lax.ppermute(other_part, "core", [(0, 1), (1, 0)])
    chip_part, own_loss = pair_rows(core, scalars, img_all, txt_all, from_other)
    scaled_late, own_loss = lax.optimization_barrier((scaled, own_loss))
    gain_t = jnp.broadcast_to(ln_gain[:, None], (WIDE, ROWS))
    gs_t = gain_t * scaled_late.T
    hidden_late, gs_t = lax.optimization_barrier((hidden, gs_t))
    hidden_other = lax.ppermute(hidden_late, "ylo", [(0, 1), (1, 0)])
    ylo = lax.axis_index("ylo")
    unit_parts = lax.all_to_all(
        chip_part, ("ylo", "yhi"), split_axis=0, concat_axis=0, tiled=True
    )
    grad_unit = jnp.sum(unit_parts.reshape(8, IMG, WIDE).astype(jnp.float32), axis=0)
    tangent = jnp.sum(img_unit * grad_unit, axis=1, keepdims=True)
    grad_low = ((grad_unit - img_unit * tangent) / img_norm).astype(jnp.bfloat16)
    loss_part = jnp.sum(other_loss + own_loss, axis=0)
    loss_block = jnp.pad(pieces(loss_part, 3), ((0, IMG - 3), (0, 0)))
    grad_send = jnp.concatenate([grad_low, loss_block], axis=1)
    grad_send, hidden_other = lax.optimization_barrier((grad_send, hidden_other))
    grad_chips = lax.all_to_all(
        jnp.broadcast_to(grad_send[None], (8, IMG, WIDE + EXTRA)).reshape(ROWS, WIDE + EXTRA),
        ("ylo", "yhi"),
        split_axis=0,
        concat_axis=0,
        tiled=True,
    )
    grad_all = lax.all_gather(grad_chips, "core", axis=0, tiled=True).reshape(
        2, 8, IMG, WIDE + EXTRA
    )
    send, own_blocks, own_sums = back_rows(
        where, grad_all, w_down, preact, w_up, gain_t, gs_t
    )
    grad_late, send = lax.optimization_barrier((grad_all, send))
    down_send = down_block(ylo, grad_late, hidden, hidden_other)
    down_got = lax.all_to_all(down_send, ("x", "z"), split_axis=0, concat_axis=0, tiled=True)
    got = lax.ppermute(send, "core", [(0, 1), (1, 0)])
    sends = chip_rows(where, own_blocks, own_sums, got)
    gots = [lax.ppermute(sends[step - 1], "yhi", turn(step)) for step in (2, 1, 3)]
    gain_own = lax.dynamic_slice_in_dim(ln_gain, col0, SLICE, 0)
    scaled_own = ((pooled.astype(jnp.float32) - average) * inverse).T
    inverse_t = jnp.broadcast_to(inverse.reshape(1, ROWS), (8, ROWS))
    grad_own = (
        lax.dynamic_slice(grad_all, (0, ylo * 4, 0, col0), (2, 4, IMG, SLICE))
        .transpose(1, 0, 2, 3)
        .reshape(ROWS, SLICE)
    )
    grad_pooled, grad_down, loss = last_rows(
        sends[3], sends[4], gots, inverse_t, inverse_t[:1] * gain_own[:, None],
        inverse_t[:1] * scaled_own, grad_own.T, down_got,
    )
    return (loss.reshape(1), grad_pooled.T, grad_down.T)


def solution(mesh):
    inner = Mesh(mesh.devices.reshape(4, 8, 2, 4, 2), DATA + TENS)
    placed = (
        P(DATA, TENS),
        P(),
        P(),
        P(None, TENS),
        P(TENS),
        P(TENS, None),
        P(TENS),
        P(DATA, TENS),
        P(DATA),
        P(DATA),
        P(),
        P(),
        P(),
    )
    return jax.shard_map(
        shards,
        mesh=inner,
        in_specs=placed,
        out_specs=(P(), P(DATA, TENS), P(TENS, DATA)),
        check_vma=False,
    )
```
